128 devices in a mesh: box: 16 (over z, x), dir: 8 (over y, core).
Axes of the slice: x: 4, y: 4, z: 4, core: 2. Of those that a mesh axis runs over, the one named last changes fastest.
Arguments:
- currents: bfloat16 [2, 3072, 128, 256], P(None, ('box', 'dir')), may hold values from -6 to 6
- near_tiles: bfloat16 [3072, 9, 2, 128, 128], P(('box', 'dir')), may hold values from -0.125 to 0.125
- near_index: int32 [3072, 9], P(('box', 'dir')), may hold values from 0 to 3071, as said below
- near_count: int32 [3072], P(('box', 'dir')), may hold values from 2 to 9
- radiate: bfloat16 [3072, 2, 128, 128], P(('box', 'dir')), may hold values from -0.375 to 0.375
- receive: bfloat16 [3072, 2, 128, 128], P(('box', 'dir')), may hold values from -0.375 to 0.375
- interp: bfloat16 [512, 128], replicated, may hold values from -0.1875 to 0.1875
- shift_angle: float32 [8, 512], replicated, may hold values from -3.140625 to 3.140625
- far_index: int32 [384, 48], replicated, may hold values from 0 to 383, as said below
- far_count: int32 [384], replicated, may hold values from 12 to 48
- trans_index: int32 [384, 48], replicated, may hold values from 0 to 315
- translators: float32 [316, 2, 512], P(None, None, ('box', 'dir')), may hold values from -0.625 to 0.625
Outputs:
- response: bfloat16 [2, 3072, 128, 256], P(None, ('box', 'dir'))
The draws below stay inside these ranges and needn't reach their ends.
Inputs may be any that keep to these rules, and one draw needn't show every extreme that they name: `near_index`: slot 0 of box b is b itself; every entry lies within 12 of its own box's index. `far_index`: no parent box lists itself.
All inputs are finite; a program needn't handle non-finite values.
Results may differ from the reference program's by a relative error of at most 0.007.
Values may be sent and summed in bfloat16 or wider, within the bound.
No kernel may reach another device: no remote copies, remote signals or barrier semaphores. Data moves between devices by JAX's collectives and lax.ppermute only.
A program may use at most 256 MiB of HBM per device.

```python
import jax
import jax.numpy as jnp
from jax import lax

P_SIZE = 128
K_A = 128
K_B = 512
NEAR = 9
FAR = 48
NOFF = 316
BOX_DEV = 24
NRHS = 256
NB = 3072
PARENTS = 384
REACH = 12


def draw_near_index(key, part):
    key = jax.random.fold_in(key, 11)
    own = jnp.arange(NB, dtype=jnp.int32)[:, None]
    offset = jax.random.randint(key, (NB, NEAR), -REACH, REACH + 1, dtype=jnp.int32)
    chosen = jnp.clip(own + offset, 0, NB - 1)
    slot_ids = jnp.arange(NEAR, dtype=jnp.int32)[None, :]
    return jnp.where(slot_ids == 0, own, chosen).astype(jnp.int32)


def draw_far_index(key, part):
    key = jax.random.fold_in(key, 23)
    own = jnp.arange(PARENTS, dtype=jnp.int32)[:, None]
    offset = jax.random.randint(key, (PARENTS, FAR), 1, PARENTS, dtype=jnp.int32)
    return ((own + offset) % PARENTS).astype(jnp.int32)


def plant(drawn, stream_key, low, top_value):
    dims = drawn.shape
    place = [jax.random.randint(jax.random.fold_in(stream_key, axis), (), 0, dims[axis]) for axis in range(len(dims))]
    drawn = drawn.at[tuple(place)].set(low)
    longest = dims.index(max(dims))
    place[longest] = (place[longest] + 1) % dims[longest]
    return drawn.at[tuple(place)].set(top_value)


def block_levels(rng, extent, split, least, high):
    gain = 1.0
    for position, parts in split:
        heights = jax.random.uniform(jax.random.fold_in(jax.random.fold_in(rng, 6), position), (parts,), jnp.float32, least / len(split), high / len(split))
        gain = gain * jnp.repeat(jnp.exp(heights), extent[position] // parts).reshape((-1,) + (1,) * (len(extent) - 1 - position))
    return gain


def bell_draw(stream_key, dims, scale, bound, split=(), held_as=jnp.bfloat16):
    array = scale * jax.random.normal(stream_key, dims, jnp.float32)
    if split:
        array = array * block_levels(stream_key, dims, split, -0.22, 0.18)
    return jnp.clip(array, -bound, bound).astype(held_as)


def setup_inputs(seed: int = 0) -> dict:
    splits = jax.random.split(jax.random.key(seed), 13)
    currents = bell_draw(splits[0], (2, NB, P_SIZE, NRHS), 1.0, 6.0, ((1, 128),))
    near_tiles = bell_draw(splits[1], (NB, NEAR, 2, P_SIZE, P_SIZE), (2 * P_SIZE * NEAR) ** -0.5, 0.125, ((0, 128),))
    near_index = draw_near_index(jax.random.fold_in(splits[12], 71), 0)
    near_count = plant(jax.random.randint(splits[3], (NB,), 2, NEAR + 1), jax.random.fold_in(splits[3], 1), 2, NEAR).astype(jnp.int32)
    radiate = bell_draw(splits[4], (NB, 2, K_A, P_SIZE), (2 * P_SIZE) ** -0.5, 0.375, ((0, 128),))
    receive = bell_draw(splits[5], (NB, 2, P_SIZE, K_A), (2 * K_A) ** -0.5, 0.375, ((0, 128),))
    interp = bell_draw(splits[6], (K_B, K_A), (8 * K_A) ** -0.5, 0.1875)
    shift_angle = jnp.clip(jax.random.uniform(splits[7], (8, K_B), jnp.float32, -3.140625, 3.140625), -3.140625, 3.140625)
    far_index = draw_far_index(jax.random.fold_in(splits[12], 71), 0)
    far_count = plant(jax.random.randint(splits[9], (PARENTS,), max(1, FAR // 4), FAR + 1), jax.random.fold_in(splits[9], 1), max(1, FAR // 4), FAR).astype(jnp.int32)
    trans_index = plant(jax.random.randint(splits[10], (PARENTS, FAR), 0, NOFF), jax.random.fold_in(splits[10], 1), 0, NOFF - 1).astype(jnp.int32)
    translators = bell_draw(splits[11], (NOFF, 2, K_B), (2 * FAR) ** -0.5, 0.625, ((2, 128),), jnp.float32)
    return dict(currents=currents, near_tiles=near_tiles, near_index=near_index, near_count=near_count, radiate=radiate, receive=receive, interp=interp, shift_angle=shift_angle, far_index=far_index, far_count=far_count, trans_index=trans_index, translators=translators)


def complex_product(form, mat_real, mat_imag, vec_real, vec_imag):
    real_part = jnp.einsum(form, mat_real, vec_real) - jnp.einsum(form, mat_imag, vec_imag)
    imag_part = jnp.einsum(form, mat_real, vec_imag) + jnp.einsum(form, mat_imag, vec_real)
    return jnp.stack([real_part, imag_part])


def translate(patterns, far_index, far_count, trans_index, translators, block_size):
    total_boxes, slot_count = far_index.shape
    slot_ids = jnp.arange(slot_count, dtype=jnp.int32)

    def one_block(inputs):
        partner, counts, offsets = inputs
        live_mask = (slot_ids[None, :] < counts[:, None]).astype(jnp.float32)
        factor = translators[offsets] * live_mask[:, :, None, None]
        sources = jnp.take(patterns, partner, axis=1).astype(jnp.float32)
        real_part = jnp.sum(factor[:, :, 0, :, None] * sources[0] - factor[:, :, 1, :, None] * sources[1], axis=1)
        imag_part = jnp.sum(factor[:, :, 1, :, None] * sources[0] + factor[:, :, 0, :, None] * sources[1], axis=1)
        return jnp.stack([real_part, imag_part]).astype(jnp.bfloat16)

    groups = total_boxes // block_size
    result = lax.map(one_block, (far_index.reshape(groups, block_size, slot_count),
                                 far_count.reshape(groups, block_size),
                                 trans_index.reshape(groups, block_size, slot_count)))
    return jnp.transpose(result, (1, 0, 2, 3, 4)).reshape(2, total_boxes, patterns.shape[2], patterns.shape[3])


def reference(currents, near_tiles, near_index, near_count, radiate, receive, interp, shift_angle,
              far_index, far_count, trans_index, translators):
    groups = NB // BOX_DEV
    kids = BOX_DEV // 8
    cosine = jnp.cos(shift_angle)[None, :, :, None]
    sine = jnp.sin(shift_angle)[None, :, :, None]
    interp_wide = interp.astype(jnp.float32)

    def upward(group):
        start = group * BOX_DEV
        block_currents = lax.dynamic_slice_in_dim(currents, start, BOX_DEV, 1).astype(jnp.float32)
        block_radiate = lax.dynamic_slice_in_dim(radiate, start, BOX_DEV, 0).astype(jnp.float32)
        leaf = complex_product("bkp,bpr->bkr", block_radiate[:, 0], block_radiate[:, 1],
                               block_currents[0], block_currents[1]).astype(jnp.bfloat16)
        spread = jnp.einsum("jk,sbkr->sbjr", interp_wide, leaf.astype(jnp.float32))
        spread = spread.reshape(2, kids, 8, K_B, NRHS)
        real_part = jnp.sum(cosine * spread[0] - sine * spread[1], axis=1)
        imag_part = jnp.sum(sine * spread[0] + cosine * spread[1], axis=1)
        return jnp.stack([real_part, imag_part]).astype(jnp.bfloat16)

    parent = lax.map(upward, jnp.arange(groups, dtype=jnp.int32))
    parent = jnp.transpose(parent, (1, 0, 2, 3, 4)).reshape(2, PARENTS, K_B, NRHS)
    incoming = translate(parent, far_index, far_count, trans_index, translators, 1)
    slot_ids = jnp.arange(NEAR, dtype=jnp.int32)

    def downward(group):
        start = group * BOX_DEV
        block_in = lax.dynamic_slice_in_dim(incoming, group * kids, kids, 1).astype(jnp.float32)
        in_real = block_in[0][:, None]
        in_imag = block_in[1][:, None]
        phased = jnp.stack([cosine * in_real + sine * in_imag,
                            cosine * in_imag - sine * in_real]).astype(jnp.bfloat16)
        phased = phased.reshape(2, BOX_DEV, K_B, NRHS)
        arriving = jnp.einsum("jk,sbjr->sbkr", interp_wide, phased.astype(jnp.float32)).astype(jnp.bfloat16)
        block_receive = lax.dynamic_slice_in_dim(receive, start, BOX_DEV, 0).astype(jnp.float32)
        arriving = arriving.astype(jnp.float32)
        far_field = complex_product("bpk,bkr->bpr", block_receive[:, 0], block_receive[:, 1],
                                    arriving[0], arriving[1])
        block_index = lax.dynamic_slice_in_dim(near_index, start, BOX_DEV, 0)
        block_count = lax.dynamic_slice_in_dim(near_count, start, BOX_DEV, 0)
        live_mask = (slot_ids[None, :] < block_count[:, None]).astype(jnp.float32)
        sources = jnp.take(currents, block_index, axis=1).astype(jnp.float32) * live_mask[None, :, :, None, None]
        tiles = lax.dynamic_slice_in_dim(near_tiles, start, BOX_DEV, 0).astype(jnp.float32)
        near_field = complex_product("bspq,bsqr->bpr", tiles[:, :, 0], tiles[:, :, 1], sources[0], sources[1])
        return (near_field + far_field).astype(jnp.bfloat16)

    response = lax.map(downward, jnp.arange(groups, dtype=jnp.int32))
    return jnp.transpose(response, (1, 0, 2, 3, 4)).reshape(2, NB, P_SIZE, NRHS)
```

```python
import jax
import jax.numpy as jnp
from jax import lax
from jax.experimental import pallas as pl
from jax.experimental.pallas import tpu as pltpu
from jax.sharding import PartitionSpec as P

BF16 = jnp.bfloat16
F32 = jnp.float32
AXES = ("box", "dir")
MIB = 1 << 20
OFF = 1 << 10


def passed_along(value, axis, by):
    peers = lax.axis_size(axis)
    pairs = [(i, i + by) for i in range(peers) if 0 <= i + by < peers]
    return lax.ppermute(value, axis, pairs)


def dot(left, right):
    return jnp.dot(left, right, preferred_element_type=F32)


def embedded(real, imag):
    return jnp.concatenate(
        [jnp.concatenate([real, -imag], axis=1), jnp.concatenate([imag, real], axis=1)], axis=0
    )


def interleave(upper, lower):
    rows, columns = upper.shape
    a = upper.reshape(rows // 8, 8, columns)
    b = lower.reshape(rows // 8, 8, columns)
    first = lax.broadcasted_iota(jnp.int32, a.shape, 1) < 4
    t = jnp.where(first, a, pltpu.roll(b, 4, 1))
    u = jnp.where(first, pltpu.roll(a, 4, 1), b)
    return jnp.stack([t, u], axis=1).reshape(2 * rows, columns)


def separate(mixed):
    rows, columns = mixed.shape
    parts = mixed.reshape(rows // 16, 2, 8, columns)
    t, u = parts[:, 0], parts[:, 1]
    first = lax.broadcasted_iota(jnp.int32, t.shape, 1) < 4
    a = jnp.where(first, t, pltpu.roll(u, 4, 1))
    b = jnp.where(first, pltpu.roll(t, 4, 1), u)
    return jnp.concatenate([a, b], axis=0).reshape(rows, columns)


def upward_kernel(cur_ref, rad_ref, interp_ref, angle_ref, out_ref, w_ref, leaf_ref):
    half = interp_ref.shape[0]

    @pl.when(pl.program_id(0) == 0)
    def _():
        angle = angle_ref[...]
        cosine = jnp.cos(angle).T
        sine = jnp.sin(angle).T
        interp = interp_ref[...].astype(F32)
        for c in range(8):
            ci = (cosine[:, c : c + 1] * interp).astype(BF16)
            si = (sine[:, c : c + 1] * interp).astype(BF16)
            w_ref[:half, c * 256 : c * 256 + 128] = ci
            w_ref[:half, c * 256 + 128 : c * 256 + 256] = -si
            w_ref[half:, c * 256 : c * 256 + 128] = si
            w_ref[half:, c * 256 + 128 : c * 256 + 256] = ci

    for c in range(8):
        x = cur_ref[:, c].reshape(256, 256)
        leaf = dot(embedded(rad_ref[c, 0], rad_ref[c, 1]), x)
        leaf_ref[c * 256 : (c + 1) * 256, :] = leaf.astype(BF16)
    y = dot(w_ref[...], leaf_ref[...])
    out_ref[...] = interleave(y[:half], y[half:]).astype(BF16)


def upward(currents, radiate, interp, angle):
    parents = currents.shape[1] // 8
    directions = interp.shape[0]
    return pl.pallas_call(
        upward_kernel,
        grid=(parents,),
        in_specs=[
            pl.BlockSpec((2, 8, 128, 256), lambda p: (0, p, 0, 0)),
            pl.BlockSpec((8, 2, 128, 128), lambda p: (p, 0, 0, 0)),
            pl.BlockSpec((directions, 128), lambda p: (0, 0)),
            pl.BlockSpec((8, directions), lambda p: (0, 0)),
        ],
        out_specs=pl.BlockSpec((2 * directions, 256), lambda p: (0, p)),
        out_shape=jax.ShapeDtypeStruct((2 * directions, parents * 256), BF16),
        scratch_shapes=[
            pltpu.VMEM((2 * directions, 2048), BF16),
            pltpu.VMEM((2048, 256), BF16),
        ],
        compiler_params=pltpu.CompilerParams(vmem_limit_bytes=60 * MIB),
        cost_estimate=pl.CostEstimate(flops=5_000_000_000, bytes_accessed=7_000_000, transcendentals=0),
        name="upward",
    )(currents, radiate, interp, angle)


def operators_kernel(pair_ref, table_ref, out_ref, mask_ref):
    slots = mask_ref.shape[1] // 16

    @pl.when(pl.program_id(0) == 0)
    def _():
        row = lax.broadcasted_iota(jnp.int32, mask_ref.shape, 0) % 16
        column = lax.broadcasted_iota(jnp.int32, mask_ref.shape, 1) // slots
        mask_ref[...] = jnp.where(row == column, 1.0, 0.0)

    def picks(size, index):
        ids = lax.broadcasted_iota(jnp.int32, (size, index.shape[1]), 0)
        return jnp.where(ids == index, 1.0, 0.0).astype(BF16)

    pair = pair_ref[0]
    factor = dot(table_ref[...], picks(table_ref.shape[1], pair & (OFF - 1)))
    factor = (factor * mask_ref[...]).astype(BF16)
    block = lax.dot_general(
        factor,
        picks(out_ref.shape[2], pair >> 10),
        (((1,), (1,)), ((), ())),
        preferred_element_type=F32,
    )
    out_ref[...] = block.reshape(out_ref.shape).astype(BF16)


def operators(pairs, table):
    blocks, _, width = pairs.shape
    parents = blocks * 16
    return pl.pallas_call(
        operators_kernel,
        grid=(blocks,),
        in_specs=[
            pl.BlockSpec((1, 1, width), lambda i: (i, 0, 0)),
            pl.BlockSpec(table.shape, lambda i: (0, 0)),
        ],
        out_specs=pl.BlockSpec((8, 16, parents), lambda i: (0, i, 0)),
        out_shape=jax.ShapeDtypeStruct((8, parents, parents), BF16),
        scratch_shapes=[pltpu.VMEM((128, width), F32)],
        compiler_params=pltpu.CompilerParams(vmem_limit_bytes=60 * MIB),
        cost_estimate=pl.CostEstimate(flops=12_000_000_000, bytes_accessed=3_000_000, transcendentals=0),
        name="operators",
    )(pairs, table)


def translate_kernel(x_ref, m_ref, out_ref, xs_ref, xj_ref, ys_ref):
    devices = x_ref.shape[0] // 8
    tiles = x_ref.shape[1] // 128
    for t in range(tiles):
        xs_ref[t] = x_ref[:, t * 128 : (t + 1) * 128].astype(F32)
    for j in range(4):
        for c in range(2):
            for t in range(tiles):
                rows = (c * (tiles // 2) + t // 2) * devices
                lanes = (t % 2) * 128
                xj_ref[rows : rows + devices, lanes : lanes + 128] = xs_ref[
                    t, pl.ds(c * 4 + j, devices, stride=8), :
                ].astype(BF16)
        real, imag = m_ref[2 * j], m_ref[2 * j + 1]
        x = xj_ref[...]
        for c, row in enumerate(((real, -imag), (imag, real))):
            y = dot(jnp.concatenate(row, axis=1), x)
            for t in range(tiles):
                ys_ref[t, pl.ds(c * 4 + j, devices, stride=8), :] = y[
                    (t // 2) * devices : (t // 2 + 1) * devices, (t % 2) * 128 : (t % 2) * 128 + 128
                ]
    for t in range(tiles):
        out_ref[:, t * 128 : (t + 1) * 128] = ys_ref[t].astype(BF16)


def translate(x, matrix):
    rows, width = x.shape
    tiles = width // 128
    return pl.pallas_call(
        translate_kernel,
        in_specs=[pl.BlockSpec(memory_space=pltpu.VMEM)] * 2,
        out_specs=pl.BlockSpec(memory_space=pltpu.VMEM),
        out_shape=jax.ShapeDtypeStruct(x.shape, BF16),
        scratch_shapes=[
            pltpu.VMEM((tiles, rows, 128), F32),
            pltpu.VMEM((rows // 8 * tiles, 256), BF16),
            pltpu.VMEM((tiles, rows, 128), F32),
        ],
        compiler_params=pltpu.CompilerParams(vmem_limit_bytes=60 * MIB),
        cost_estimate=pl.CostEstimate(flops=1_200_000_000, bytes_accessed=5_500_000, transcendentals=0),
        name="translate",
    )(x, matrix)


def near_kernel(index_ref, count_ref, low_ref, cur_ref, up_ref, tile_ref, out_ref, win_ref, sems):
    step = pl.program_id(0)
    group, slots = tile_ref.shape[:2]
    reach = low_ref.shape[1]
    boxes = cur_ref.shape[1]

    @pl.when(step == 0)
    def _():
        copies = []
        for c in range(2):
            rows = pl.ds(c * 128, 128)
            starts = ((low_ref, 0, reach), (cur_ref, reach, boxes), (up_ref, reach + boxes, reach))
            for n, (source, start, size) in enumerate(starts):
                copies.append(
                    pltpu.make_async_copy(
                        source.at[c], win_ref.at[pl.ds(start, size), rows, :], sems.at[c * 3 + n]
                    )
                )
        for copy in copies:
            copy.start()
        for copy in copies:
            copy.wait()

    @pl.loop(0, group)
    def _(i):
        box = step * group + i
        for live in range(1, slots + 1):

            @pl.when(count_ref[box] == live)
            def _():
                tiles = [embedded(tile_ref[i, s, 0], tile_ref[i, s, 1]) for s in range(live)]
                picked = [win_ref[index_ref[box * slots + s]] for s in range(live)]
                out_ref[i] = dot(
                    jnp.concatenate(tiles, axis=1), jnp.concatenate(picked, axis=0)
                ).astype(out_ref.dtype)


def near(index, count, low, currents, up, tiles):
    boxes, slots = tiles.shape[:2]
    reach = low.shape[1]
    group = 4
    return pl.pallas_call(
        near_kernel,
        grid_spec=pltpu.PrefetchScalarGridSpec(
            num_scalar_prefetch=2,
            grid=(boxes // group,),
            in_specs=[
                pl.BlockSpec(memory_space=pl.ANY),
                pl.BlockSpec(memory_space=pl.ANY),
                pl.BlockSpec(memory_space=pl.ANY),
                pl.BlockSpec((group, slots, 2, 128, 128), lambda b, i, n: (b, 0, 0, 0, 0)),
            ],
            out_specs=pl.BlockSpec((group, 256, 256), lambda b, i, n: (b, 0, 0)),
            scratch_shapes=[
                pltpu.VMEM((boxes + 2 * reach, 256, 256), BF16),
                pltpu.SemaphoreType.DMA((6,)),
            ],
        ),
        out_shape=jax.ShapeDtypeStruct((boxes, 256, 256), BF16),
        compiler_params=pltpu.CompilerParams(vmem_limit_bytes=60 * MIB),
        cost_estimate=pl.CostEstimate(flops=7_200_000_000, bytes_accessed=27_000_000, transcendentals=0),
        name="near",
    )(index, count, low, currents, up, tiles)


def downward_kernel(z_ref, rec_ref, interp_ref, angle_ref, near_ref, out_ref, w_ref, arr_ref):
    half = angle_ref.shape[1]

    @pl.when(pl.program_id(0) == 0)
    def _():
        angle = angle_ref[...]
        cosine = jnp.cos(angle)
        sine = jnp.sin(angle)
        interp = interp_ref[...].astype(F32).T
        for c in range(8):
            ci = (cosine[c : c + 1] * interp).astype(BF16)
            si = (sine[c : c + 1] * interp).astype(BF16)
            w_ref[c * 256 : c * 256 + 128, :half] = ci
            w_ref[c * 256 : c * 256 + 128, half:] = si
            w_ref[c * 256 + 128 : c * 256 + 256, :half] = -si
            w_ref[c * 256 + 128 : c * 256 + 256, half:] = ci

    z = separate(z_ref[...].astype(F32)).astype(BF16)
    arr_ref[...] = dot(w_ref[...], z).astype(BF16)
    for c in range(8):
        far = dot(embedded(rec_ref[c, 0], rec_ref[c, 1]), arr_ref[c * 256 : (c + 1) * 256, :])
        out_ref[:, c] = (far + near_ref[c].astype(F32)).astype(BF16).reshape(2, 128, 256)


def downward(z, receive, interp, angle, near_field):
    boxes = receive.shape[0]
    directions = interp.shape[0]
    return pl.pallas_call(
        downward_kernel,
        grid=(boxes // 8,),
        in_specs=[
            pl.BlockSpec((2 * directions, 256), lambda p: (0, p)),
            pl.BlockSpec((8, 2, 128, 128), lambda p: (p, 0, 0, 0)),
            pl.BlockSpec((directions, 128), lambda p: (0, 0)),
            pl.BlockSpec((8, directions), lambda p: (0, 0)),
            pl.BlockSpec((8, 256, 256), lambda p: (p, 0, 0)),
        ],
        out_specs=pl.BlockSpec((2, 8, 128, 256), lambda p: (0, p, 0, 0)),
        out_shape=jax.ShapeDtypeStruct((2, boxes, 128, 256), BF16),
        scratch_shapes=[
            pltpu.VMEM((2048, 2 * directions), BF16),
            pltpu.VMEM((2048, 256), BF16),
        ],
        compiler_params=pltpu.CompilerParams(vmem_limit_bytes=60 * MIB),
        cost_estimate=pl.CostEstimate(flops=5_000_000_000, bytes_accessed=13_000_000, transcendentals=0),
        name="downward",
    )(z, receive, interp, angle, near_field)


def exchanged(value):
    return lax.all_to_all(value, AXES, split_axis=0, concat_axis=0, tiled=True)


def local(
    currents,
    near_tiles,
    near_index,
    near_count,
    radiate,
    receive,
    interp,
    shift_angle,
    far_index,
    far_count,
    trans_index,
    translators,
):
    boxes = currents.shape[1]
    reach = boxes // 2
    owned = boxes // 8
    parents, slots = far_index.shape
    devices = parents // owned
    lower = passed_along(currents[:, boxes - reach :], AXES, 1)
    upper = passed_along(currents[:, :reach], AXES, -1)

    sent = upward(currents, radiate, interp, shift_angle)
    by_direction = exchanged(sent)

    def blocks(value):
        value = value.reshape(devices, owned, slots).transpose(1, 0, 2)
        return value.reshape(parents // 16, 1, 16 * slots)

    live = jnp.arange(slots, dtype=jnp.int32)[None, :] < far_count[:, None]
    source = jnp.where(live, far_index % owned * devices + far_index // owned, OFF)
    pairs = blocks(source * OFF + trans_index)
    table = translators.transpose(2, 1, 0).reshape(8, -1).astype(BF16)
    table = jnp.pad(table, ((0, 0), (0, -table.shape[1] % 128)))
    table = jnp.repeat(table, 16, axis=0)
    matrix = operators(pairs, table)

    back = translate(by_direction, matrix)
    incoming = exchanged(back)

    first = lax.axis_index(AXES) * boxes - reach
    near_field = near(
        (near_index - first).reshape(-1), near_count, lower, currents, upper, near_tiles
    )
    return downward(incoming, receive, interp, shift_angle, near_field)


def solution(mesh):
    placed = (
        P(None, AXES, None, None),
        P(AXES, None, None, None, None),
        P(AXES, None),
        P(AXES),
        P(AXES, None, None, None),
        P(AXES, None, None, None),
        P(),
        P(),
        P(),
        P(),
        P(),
        P(None, None, AXES),
    )
    return jax.shard_map(
        local,
        mesh=mesh,
        in_specs=placed,
        out_specs=P(None, AXES, None, None),
        check_vma=False,
    )
```

```python
import jax
import jax.numpy as jnp
from jax import lax
from jax.experimental import pallas as pl
from jax.experimental.pallas import tpu as pltpu
from jax.sharding import PartitionSpec as P

BF16 = jnp.bfloat16
F32 = jnp.float32
AXES = ("box", "dir")
MIB = 1 << 20
OWNED = 3
CODE = 512
DEAD = 1023


def passed_along(value, axis, by):
    peers = lax.axis_size(axis)
    pairs = [(i, i + by) for i in range(peers) if 0 <= i + by < peers]
    return lax.ppermute(value, axis, pairs)


def dot(left, right):
    return jnp.dot(left, right, preferred_element_type=F32)


def embedded(real, imag):
    return jnp.concatenate(
        [jnp.concatenate([real, -imag], axis=1), jnp.concatenate([imag, real], axis=1)], axis=0
    )


def interleave(upper, lower):
    rows, columns = upper.shape
    a = upper.reshape(rows // 8, 8, columns)
    b = lower.reshape(rows // 8, 8, columns)
    first = lax.broadcasted_iota(jnp.int32, a.shape, 1) < 4
    t = jnp.where(first, a, pltpu.roll(b, 4, 1))
    u = jnp.where(first, pltpu.roll(a, 4, 1), b)
    return jnp.stack([t, u], axis=1).reshape(2 * rows, columns)


def separate(mixed):
    rows, columns = mixed.shape
    parts = mixed.reshape(rows // 16, 2, 8, columns)
    t, u = parts[:, 0], parts[:, 1]
    first = lax.broadcasted_iota(jnp.int32, t.shape, 1) < 4
    a = jnp.where(first, t, pltpu.roll(u, 4, 1))
    b = jnp.where(first, pltpu.roll(t, 4, 1), u)
    return jnp.concatenate([a, b], axis=0).reshape(rows, columns)


def upward_kernel(
    cur_hbm, rad_hbm, interp_ref, angle_ref, out_hbm, first_hbm, last_hbm,
    cur_ref, rad_ref, w_ref, leaf_ref, out_ref, in_sems, halo_sems, out_sems
):
    half = interp_ref.shape[0]
    boxes = cur_ref.shape[1]
    parents = boxes // 8
    reach = first_hbm.shape[1]
    pieces = out_sems.shape[1]
    piece = half // pieces

    def arrivals(p):
        of = pl.ds(p * 8, 8)
        return (
            pltpu.make_async_copy(cur_hbm.at[:, of], cur_ref.at[:, of], in_sems.at[p, 0]),
            pltpu.make_async_copy(rad_hbm.at[of], rad_ref.at[of], in_sems.at[p, 1]),
        )

    for copy in arrivals(0):
        copy.start()

    angle = angle_ref[...]
    cosine = jnp.cos(angle).T
    sine = jnp.sin(angle).T
    interp = interp_ref[...].astype(F32)
    for c in range(8):
        ci = (cosine[:, c : c + 1] * interp).astype(BF16)
        si = (sine[:, c : c + 1] * interp).astype(BF16)
        left = slice(c * 256, c * 256 + 128)
        right = slice(c * 256 + 128, c * 256 + 256)
        for n in range(pieces):
            rows = slice(n * piece, (n + 1) * piece)
            real = slice(2 * n * piece, (2 * n + 1) * piece)
            imag = slice((2 * n + 1) * piece, (2 * n + 2) * piece)
            w_ref[real, left] = ci[rows]
            w_ref[real, right] = -si[rows]
            w_ref[imag, left] = si[rows]
            w_ref[imag, right] = ci[rows]

    def departures(p):
        lanes = pl.ds(pl.multiple_of(p * 256, 256), 256)
        copies = []
        for n in range(pieces):
            rows = pl.ds(2 * n * piece, 2 * piece)
            copies.append(
                pltpu.make_async_copy(
                    out_ref.at[p, rows], out_hbm.at[rows, lanes], out_sems.at[p, n]
                )
            )
        return copies

    halos = []
    for n, (start, target) in enumerate(((0, first_hbm), (boxes - reach, last_hbm))):
        source = cur_ref.at[:, pl.ds(start, reach)]
        halos.append(pltpu.make_async_copy(source, target, halo_sems.at[n]))

    def body(p, carry):
        for copy in arrivals(p):
            copy.wait()

        @pl.when(p + 1 < parents)
        def _():
            for copy in arrivals(p + 1):
                copy.start()

        @pl.when(p + 1 == parents)
        def _():
            for copy in halos:
                copy.start()

        for c in range(8):
            box = p * 8 + c
            x = cur_ref[:, box].reshape(256, 256)
            leaf = dot(embedded(rad_ref[box, 0], rad_ref[box, 1]), x)
            leaf_ref[c * 256 : (c + 1) * 256, :] = leaf.astype(BF16)
        for n, copy in enumerate(departures(p)):
            rows = slice(2 * n * piece, (2 * n + 2) * piece)
            y = dot(w_ref[rows], leaf_ref[...])
            out_ref[p, rows, :] = interleave(y[:piece], y[piece:]).astype(BF16)
            copy.start()
        return carry

    lax.fori_loop(0, parents, body, 0)
    for p in range(parents):
        for copy in departures(p):
            copy.wait()
    for copy in halos:
        copy.wait()


def upward(currents, radiate, interp, angle):
    parts, boxes, unknowns, columns = currents.shape
    parents = boxes // 8
    directions = interp.shape[0]
    sent = (2 * directions, parents * columns)
    halo = jax.ShapeDtypeStruct((parts, boxes // 2, unknowns, columns), BF16)
    return pl.pallas_call(
        upward_kernel,
        in_specs=[
            pl.BlockSpec(memory_space=pltpu.HBM),
            pl.BlockSpec(memory_space=pltpu.HBM),
            pl.BlockSpec(memory_space=pltpu.VMEM),
            pl.BlockSpec(memory_space=pltpu.VMEM),
        ],
        out_specs=[pl.BlockSpec(memory_space=pl.ANY)] * 3,
        out_shape=[jax.ShapeDtypeStruct(sent, BF16), halo, halo],
        scratch_shapes=[
            pltpu.VMEM(currents.shape, BF16),
            pltpu.VMEM(radiate.shape, BF16),
            pltpu.VMEM((2 * directions, 2048), BF16),
            pltpu.VMEM((2048, 256), BF16),
            pltpu.VMEM((parents, 2 * directions, columns), BF16),
            pltpu.SemaphoreType.DMA((parents, 2)),
            pltpu.SemaphoreType.DMA((2,)),
            pltpu.SemaphoreType.DMA((parents, 2)),
        ],
        compiler_params=pltpu.CompilerParams(vmem_limit_bytes=60 * MIB),
        cost_estimate=pl.CostEstimate(flops=5_000_000_000, bytes_accessed=7_000_000, transcendentals=0),
        name="upward",
    )(currents, radiate, interp, angle)


def iota(shape, axis):
    return lax.broadcasted_iota(jnp.int32, shape, axis)


def operators_kernel(far_ref, trans_ref, count_ref, table_ref, out_ref, code_ref, wide_ref, mask_ref):
    slots, parents = far_ref.shape
    blocks, width = code_ref.shape
    owned = OWNED
    devices = parents // owned
    per = blocks // owned

    def device(p):
        return (p * (65536 // owned + 1)) >> 16

    far = far_ref[...]
    source = (far - device(far) * owned) * devices + device(far)
    live = iota(far.shape, 0) < count_ref[...]
    code = jnp.where(live, source, DEAD) * CODE + trans_ref[...]
    lane = iota((1, width), 1)
    owner = lane // slots
    spread = jnp.where(iota((slots, width), 0) == lane - owner * slots, 1.0, 0.0)
    exact = dict(precision=lax.Precision.HIGHEST, preferred_element_type=F32)
    flat = jnp.dot(code.astype(F32).T, spread, **exact)
    flat = jnp.where((device(iota((parents, 1), 0)) & 15) == owner, flat, 0.0)
    p = iota((1, parents), 1)
    block = (p - device(p) * owned) * per + (device(p) >> 4)
    member = jnp.where(iota((blocks, parents), 0) == block, 1.0, 0.0)
    code_ref[...] = jnp.dot(member, flat, **exact).astype(jnp.int32)
    table = table_ref[...]
    wide = jnp.broadcast_to(table[:, None, :], (8, 16, table.shape[1]))
    wide_ref[...] = wide.reshape(128, table.shape[1]).astype(BF16)
    mask_ref[...] = jnp.where((iota((128, 1), 0) & 15) == owner, 1.0, 0.0).astype(BF16)

    def picks(size, index):
        return jnp.where(iota((size, width), 0) == index, 1.0, 0.0).astype(BF16)

    def body(i, carry):
        code = code_ref[pl.ds(i, 1), :]
        factor = dot(wide_ref[...], picks(wide_ref.shape[1], code & (CODE - 1)))
        factor = factor.astype(BF16) * mask_ref[...]
        matrix = lax.dot_general(
            factor,
            picks(parents, code >> 9),
            (((1,), (1,)), ((), ())),
            preferred_element_type=F32,
        )
        rows = pl.ds(pl.multiple_of(i * 16, 16), 16)
        out_ref[:, rows, :] = matrix.reshape(8, 16, parents).astype(BF16)
        return carry

    lax.fori_loop(0, blocks, body, 0, unroll=2)


def operators(far, trans, count, table):
    slots, parents = far.shape
    blocks = parents // 16
    return pl.pallas_call(
        operators_kernel,
        in_specs=[pl.BlockSpec(memory_space=pltpu.VMEM)] * 4,
        out_specs=pl.BlockSpec(memory_space=pltpu.VMEM),
        out_shape=jax.ShapeDtypeStruct((8, parents, parents), BF16),
        scratch_shapes=[
            pltpu.VMEM((blocks, 16 * slots), jnp.int32),
            pltpu.VMEM((128, table.shape[1]), BF16),
            pltpu.VMEM((128, 16 * slots), BF16),
        ],
        compiler_params=pltpu.CompilerParams(vmem_limit_bytes=32 * MIB),
        cost_estimate=pl.CostEstimate(flops=12_000_000_000, bytes_accessed=3_000_000, transcendentals=0),
        name="operators",
    )(far, trans, count, table)


def translate_kernel(x_hbm, m_ref, out_ref, x_ref, xp_ref, yp_ref, sems):
    groups = 4
    rows = x_ref.shape[0] // groups
    share = rows // 8
    owned = x_ref.shape[1] // 256
    parents = m_ref.shape[1]
    copies = []
    for g in range(groups):
        of = pl.ds(g * rows, rows)
        copies.append(pltpu.make_async_copy(x_hbm.at[of], x_ref.at[of], sems.at[g]))
    copies[0].start()
    copies[1].start()
    row, column = iota((rows, rows), 0), iota((rows, rows), 1)
    gather = jnp.where(column == (row & (share - 1)) * 8 + (row // share), 1.0, 0.0).astype(BF16)
    scatter = jnp.where(column == (row & 7) * share + (row >> 3), 1.0, 0.0).astype(BF16)
    for g in range(groups):
        copies[g].wait()
        if g + 2 < groups:
            copies[g + 2].start()
        xp_ref[g] = dot(gather, x_ref[g * rows : (g + 1) * rows, :]).astype(BF16)
    for j in range(4):
        x = jnp.concatenate(
            [
                xp_ref[g, (c * 4 + j) * share : (c * 4 + j + 1) * share, p * 256 : (p + 1) * 256]
                for c in range(2)
                for p in range(owned)
                for g in range(groups)
            ],
            axis=0,
        )
        y = dot(embedded(m_ref[2 * j], m_ref[2 * j + 1]), x).astype(BF16)
        for c in range(2):
            for p in range(owned):
                for g in range(groups):
                    start = c * parents + (p * groups + g) * share
                    yp_ref[
                        g, (c * 4 + j) * share : (c * 4 + j + 1) * share, p * 256 : (p + 1) * 256
                    ] = y[start : start + share]
    for g in range(groups):
        out_ref[g * rows : (g + 1) * rows, :] = dot(scatter, yp_ref[g]).astype(BF16)


def translate(x, matrix):
    rows, width = x.shape
    return pl.pallas_call(
        translate_kernel,
        in_specs=[pl.BlockSpec(memory_space=pltpu.HBM), pl.BlockSpec(memory_space=pltpu.VMEM)],
        out_specs=pl.BlockSpec(memory_space=pltpu.VMEM),
        out_shape=jax.ShapeDtypeStruct(x.shape, BF16),
        scratch_shapes=[
            pltpu.VMEM(x.shape, BF16),
            pltpu.VMEM((4, rows // 4, width), BF16),
            pltpu.VMEM((4, rows // 4, width), BF16),
            pltpu.SemaphoreType.DMA((4,)),
        ],
        compiler_params=pltpu.CompilerParams(vmem_limit_bytes=32 * MIB),
        cost_estimate=pl.CostEstimate(flops=1_200_000_000, bytes_accessed=5_500_000, transcendentals=0),
        name="translate",
    )(pltpu.with_memory_space_constraint(x, pltpu.HBM), matrix)


def near_kernel(index_ref, count_ref, low_ref, cur_ref, up_ref, tile_ref, out_ref, win_ref, sems):
    step = pl.program_id(0)
    group, slots = tile_ref.shape[:2]
    reach = low_ref.shape[1]
    boxes = cur_ref.shape[1]

    @pl.when(step == 0)
    def _():
        copies = []
        for c in range(2):
            rows = pl.ds(c * 128, 128)
            starts = ((low_ref, 0, reach), (cur_ref, reach, boxes), (up_ref, reach + boxes, reach))
            for n, (source, start, size) in enumerate(starts):
                copies.append(
                    pltpu.make_async_copy(
                        source.at[c], win_ref.at[pl.ds(start, size), rows, :], sems.at[c * 3 + n]
                    )
                )
        for copy in copies:
            copy.start()
        for copy in copies:
            copy.wait()

    @pl.loop(0, group)
    def _(i):
        box = step * group + i
        for live in range(1, slots + 1):

            @pl.when(count_ref[box] == live)
            def _():
                tiles = [embedded(tile_ref[i, s, 0], tile_ref[i, s, 1]) for s in range(live)]
                picked = [win_ref[index_ref[box * slots + s]] for s in range(live)]
                out_ref[i] = dot(
                    jnp.concatenate(tiles, axis=1), jnp.concatenate(picked, axis=0)
                ).astype(out_ref.dtype)


def near(index, count, low, currents, up, tiles):
    boxes, slots = tiles.shape[:2]
    reach = low.shape[1]
    group = 4
    return pl.pallas_call(
        near_kernel,
        grid_spec=pltpu.PrefetchScalarGridSpec(
            num_scalar_prefetch=2,
            grid=(boxes // group,),
            in_specs=[
                pl.BlockSpec(memory_space=pl.ANY),
                pl.BlockSpec(memory_space=pl.ANY),
                pl.BlockSpec(memory_space=pl.ANY),
                pl.BlockSpec((group, slots, 2, 128, 128), lambda b, i, n: (b, 0, 0, 0, 0)),
            ],
            out_specs=pl.BlockSpec((group, 256, 256), lambda b, i, n: (b, 0, 0)),
            scratch_shapes=[
                pltpu.VMEM((boxes + 2 * reach, 256, 256), BF16),
                pltpu.SemaphoreType.DMA((6,)),
            ],
        ),
        out_shape=pltpu.HBM((boxes, 256, 256), BF16),
        compiler_params=pltpu.CompilerParams(vmem_limit_bytes=60 * MIB),
        cost_estimate=pl.CostEstimate(flops=7_200_000_000, bytes_accessed=27_000_000, transcendentals=0),
        name="near",
    )(index, count, low, currents, up, tiles)


def downward_kernel(
    z_ref, interp_ref, angle_ref, rec_hbm, near_hbm, out_hbm,
    rec_ref, near_ref, w_ref, arr_ref, out_ref, in_sems, out_sems
):
    half = angle_ref.shape[1]
    parents = z_ref.shape[1] // 256
    coming = []
    for p in range(parents):
        of = pl.ds(p * 8, 8)
        coming.append(
            (
                pltpu.make_async_copy(rec_hbm.at[of], rec_ref.at[of], in_sems.at[p, 0]),
                pltpu.make_async_copy(near_hbm.at[of], near_ref.at[of], in_sems.at[p, 1]),
            )
        )
    for copy in coming[0]:
        copy.start()
    angle = angle_ref[...]
    cosine = jnp.cos(angle)
    sine = jnp.sin(angle)
    interp = interp_ref[...].astype(F32).T

    def matrix(c):
        ci = (cosine[c : c + 1] * interp).astype(BF16)
        si = (sine[c : c + 1] * interp).astype(BF16)
        w_ref[c * 256 : c * 256 + 128, :half] = ci
        w_ref[c * 256 : c * 256 + 128, half:] = si
        w_ref[c * 256 + 128 : c * 256 + 256, :half] = -si
        w_ref[c * 256 + 128 : c * 256 + 256, half:] = ci

    going = []
    for p in range(parents):
        z = separate(z_ref[:, p * 256 : (p + 1) * 256].astype(F32)).astype(BF16)
        pieces = 4 if p == 0 else 1
        for n in range(pieces):
            if p == 0:
                for c in range(n * 8 // pieces, (n + 1) * 8 // pieces):
                    matrix(c)
            rows = slice(n * 2048 // pieces, (n + 1) * 2048 // pieces)
            arr_ref[p % 2, rows, :] = dot(w_ref[rows, :], z).astype(BF16)
        for copy in coming[p]:
            copy.wait()
        if p + 1 < parents:
            for copy in coming[p + 1]:
                copy.start()
        for c in range(8):
            box = p * 8 + c
            arriving = arr_ref[p % 2, c * 256 : (c + 1) * 256, :]
            far = dot(embedded(rec_ref[box, 0], rec_ref[box, 1]), arriving)
            out_ref[:, box] = (far + near_ref[box].astype(F32)).astype(BF16).reshape(2, 128, 256)
            if c % 4 == 3:
                of = pl.ds(box - 3, 4)
                going.append(
                    pltpu.make_async_copy(
                        out_ref.at[:, of], out_hbm.at[:, of], out_sems.at[box // 4]
                    )
                )
                going[-1].start()
    for copy in going:
        copy.wait()


def downward(z, interp, angle, receive, near_field):
    boxes = receive.shape[0]
    response = (2, boxes, 128, 256)
    return pl.pallas_call(
        downward_kernel,
        in_specs=[pl.BlockSpec(memory_space=pltpu.VMEM)] * 3
        + [pl.BlockSpec(memory_space=pltpu.HBM)] * 2,
        out_specs=pl.BlockSpec(memory_space=pltpu.HBM),
        out_shape=jax.ShapeDtypeStruct(response, BF16),
        scratch_shapes=[
            pltpu.VMEM(receive.shape, BF16),
            pltpu.VMEM(near_field.shape, BF16),
            pltpu.VMEM((2048, 2 * interp.shape[0]), BF16),
            pltpu.VMEM((2, 2048, 256), BF16),
            pltpu.VMEM(response, BF16),
            pltpu.SemaphoreType.DMA((boxes // 8, 2)),
            pltpu.SemaphoreType.DMA((boxes // 4,)),
        ],
        compiler_params=pltpu.CompilerParams(vmem_limit_bytes=32 * MIB),
        cost_estimate=pl.CostEstimate(flops=5_000_000_000, bytes_accessed=13_000_000, transcendentals=0),
        name="downward",
    )(
        z,
        interp,
        angle,
        pltpu.with_memory_space_constraint(receive, pltpu.HBM),
        pltpu.with_memory_space_constraint(near_field, pltpu.HBM),
    )


def exchanged(value):
    return lax.all_to_all(value, AXES, split_axis=0, concat_axis=0, tiled=True)


def local(
    currents,
    near_tiles,
    near_index,
    near_count,
    radiate,
    receive,
    interp,
    shift_angle,
    far_index,
    far_count,
    trans_index,
    translators,
):
    boxes = currents.shape[1]
    reach = boxes // 2
    sent, leading, trailing = upward(currents, radiate, interp, shift_angle)
    by_direction = exchanged(sent)
    lower = passed_along(trailing, AXES, 1)
    upper = passed_along(leading, AXES, -1)

    table = translators.transpose(2, 1, 0).reshape(8, -1)
    table = jnp.pad(table, ((0, 0), (0, -table.shape[1] % 128)))
    matrix = operators(far_index.T, trans_index.T, far_count[None, :], table)

    back = translate(by_direction, matrix)
    incoming = exchanged(back)

    first = lax.axis_index(AXES) * boxes - reach
    near_field = near(
        (near_index - first).reshape(-1), near_count, lower, currents, upper, near_tiles
    )
    return downward(incoming, interp, shift_angle, receive, near_field)


def solution(mesh):
    placed = (
        P(None, AXES, None, None),
        P(AXES, None, None, None, None),
        P(AXES, None),
        P(AXES),
        P(AXES, None, None, None),
        P(AXES, None, None, None),
        P(),
        P(),
        P(),
        P(),
        P(),
        P(None, None, AXES),
    )
    return jax.shard_map(
        local,
        mesh=mesh,
        in_specs=placed,
        out_specs=P(None, AXES, None, None),
        check_vma=False,
    )
```

```python
import jax
import jax.numpy as jnp
from jax import lax
from jax.experimental import pallas as pl
from jax.experimental.pallas import tpu as pltpu
from jax.sharding import PartitionSpec as P

BF16 = jnp.bfloat16
F32 = jnp.float32
AXES = ("box", "dir")
MIB = 1 << 20
OWNED = 3
CODE = 512
DEAD = 1023


def passed_along(value, axis, by):
    peers = lax.axis_size(axis)
    pairs = [(i, i + by) for i in range(peers) if 0 <= i + by < peers]
    return lax.ppermute(value, axis, pairs)


def dot(left, right):
    return jnp.dot(left, right, preferred_element_type=F32)


def embedded(real, imag):
    return jnp.concatenate(
        [jnp.concatenate([real, -imag], axis=1), jnp.concatenate([imag, real], axis=1)], axis=0
    )


def interleave(upper, lower):
    rows, columns = upper.shape
    a = upper.reshape(rows // 8, 8, columns)
    b = lower.reshape(rows // 8, 8, columns)
    first = lax.broadcasted_iota(jnp.int32, a.shape, 1) < 4
    t = jnp.where(first, a, pltpu.roll(b, 4, 1))
    u = jnp.where(first, pltpu.roll(a, 4, 1), b)
    return jnp.stack([t, u], axis=1).reshape(2 * rows, columns)


def separate(mixed):
    rows, columns = mixed.shape
    parts = mixed.reshape(rows // 16, 2, 8, columns)
    t, u = parts[:, 0], parts[:, 1]
    first = lax.broadcasted_iota(jnp.int32, t.shape, 1) < 4
    a = jnp.where(first, t, pltpu.roll(u, 4, 1))
    b = jnp.where(first, pltpu.roll(t, 4, 1), u)
    return jnp.concatenate([a, b], axis=0).reshape(rows, columns)


def upward_kernel(
    cur_hbm, rad_hbm, interp_ref, angle_ref, out_hbm, first_hbm, last_hbm,
    cur_ref, rad_ref, w_ref, leaf_ref, out_ref, in_sems, halo_sems, out_sems
):
    half = interp_ref.shape[0]
    boxes = cur_ref.shape[1]
    parents = boxes // 8
    reach = first_hbm.shape[1]
    pieces = out_sems.shape[1]
    piece = half // pieces

    def arrivals(p):
        of = pl.ds(p * 8, 8)
        return (
            pltpu.make_async_copy(cur_hbm.at[:, of], cur_ref.at[:, of], in_sems.at[p, 0]),
            pltpu.make_async_copy(rad_hbm.at[of], rad_ref.at[of], in_sems.at[p, 1]),
        )

    for copy in arrivals(0):
        copy.start()

    angle = angle_ref[...]
    cosine = jnp.cos(angle).T
    sine = jnp.sin(angle).T
    interp = interp_ref[...].astype(F32)
    for c in range(8):
        ci = (cosine[:, c : c + 1] * interp).astype(BF16)
        si = (sine[:, c : c + 1] * interp).astype(BF16)
        left = slice(c * 256, c * 256 + 128)
        right = slice(c * 256 + 128, c * 256 + 256)
        for n in range(pieces):
            rows = slice(n * piece, (n + 1) * piece)
            real = slice(2 * n * piece, (2 * n + 1) * piece)
            imag = slice((2 * n + 1) * piece, (2 * n + 2) * piece)
            w_ref[real, left] = ci[rows]
            w_ref[real, right] = -si[rows]
            w_ref[imag, left] = si[rows]
            w_ref[imag, right] = ci[rows]

    def departures(p):
        lanes = pl.ds(pl.multiple_of(p * 256, 256), 256)
        copies = []
        for n in range(pieces):
            rows = pl.ds(2 * n * piece, 2 * piece)
            copies.append(
                pltpu.make_async_copy(
                    out_ref.at[p, rows], out_hbm.at[rows, lanes], out_sems.at[p, n]
                )
            )
        return copies

    halos = []
    for n, (start, target) in enumerate(((0, first_hbm), (boxes - reach, last_hbm))):
        source = cur_ref.at[:, pl.ds(start, reach)]
        halos.append(pltpu.make_async_copy(source, target, halo_sems.at[n]))

    def body(p, carry):
        for copy in arrivals(p):
            copy.wait()

        @pl.when(p + 1 < parents)
        def _():
            for copy in arrivals(p + 1):
                copy.start()

        @pl.when(p + 1 == parents)
        def _():
            for copy in halos:
                copy.start()

        for c in range(8):
            box = p * 8 + c
            x = cur_ref[:, box].reshape(256, 256)
            leaf = dot(embedded(rad_ref[box, 0], rad_ref[box, 1]), x)
            leaf_ref[c * 256 : (c + 1) * 256, :] = leaf.astype(BF16)
        for n, copy in enumerate(departures(p)):
            rows = slice(2 * n * piece, (2 * n + 2) * piece)
            y = dot(w_ref[rows], leaf_ref[...])
            out_ref[p, rows, :] = interleave(y[:piece], y[piece:]).astype(BF16)
            copy.start()
        return carry

    lax.fori_loop(0, parents, body, 0)
    for p in range(parents):
        for copy in departures(p):
            copy.wait()
    for copy in halos:
        copy.wait()


def upward(currents, radiate, interp, angle):
    parts, boxes, unknowns, columns = currents.shape
    parents = boxes // 8
    directions = interp.shape[0]
    sent = (2 * directions, parents * columns)
    halo = jax.ShapeDtypeStruct((parts, boxes // 2, unknowns, columns), BF16)
    return pl.pallas_call(
        upward_kernel,
        in_specs=[
            pl.BlockSpec(memory_space=pltpu.HBM),
            pl.BlockSpec(memory_space=pltpu.HBM),
            pl.BlockSpec(memory_space=pltpu.VMEM),
            pl.BlockSpec(memory_space=pltpu.VMEM),
        ],
        out_specs=[pl.BlockSpec(memory_space=pl.ANY)] * 3,
        out_shape=[jax.ShapeDtypeStruct(sent, BF16), halo, halo],
        scratch_shapes=[
            pltpu.VMEM(currents.shape, BF16),
            pltpu.VMEM(radiate.shape, BF16),
            pltpu.VMEM((2 * directions, 2048), BF16),
            pltpu.VMEM((2048, 256), BF16),
            pltpu.VMEM((parents, 2 * directions, columns), BF16),
            pltpu.SemaphoreType.DMA((parents, 2)),
            pltpu.SemaphoreType.DMA((2,)),
            pltpu.SemaphoreType.DMA((parents, 2)),
        ],
        compiler_params=pltpu.CompilerParams(vmem_limit_bytes=60 * MIB),
        cost_estimate=pl.CostEstimate(flops=5_000_000_000, bytes_accessed=7_000_000, transcendentals=0),
        name="upward",
    )(currents, radiate, interp, angle)


def iota(shape, axis):
    return lax.broadcasted_iota(jnp.int32, shape, axis)


def operators_kernel(
    far_ref, trans_ref, count_ref, table_ref, out_ref, rest_hbm, code_ref, wide_ref, mask_ref, rest_ref, sem
):
    slots, parents = far_ref.shape
    blocks, width = code_ref.shape
    owned = OWNED
    devices = parents // owned
    per = blocks // owned

    def device(p):
        return (p * (65536 // owned + 1)) >> 16

    far = far_ref[...]
    source = (far - device(far) * owned) * devices + device(far)
    live = iota(far.shape, 0) < count_ref[...]
    code = jnp.where(live, source, DEAD) * CODE + trans_ref[...]
    lane = iota((1, width), 1)
    owner = lane // slots
    spread = jnp.where(iota((slots, width), 0) == lane - owner * slots, 1.0, 0.0)
    exact = dict(precision=lax.Precision.HIGHEST, preferred_element_type=F32)
    flat = jnp.dot(code.astype(F32).T, spread, **exact)
    flat = jnp.where((device(iota((parents, 1), 0)) & 15) == owner, flat, 0.0)
    p = iota((1, parents), 1)
    block = (p - device(p) * owned) * per + (device(p) >> 4)
    member = jnp.where(iota((blocks, parents), 0) == block, 1.0, 0.0)
    code_ref[...] = jnp.dot(member, flat, **exact).astype(jnp.int32)
    table = table_ref[...]
    wide = jnp.broadcast_to(table[:, None, :], (8, 16, table.shape[1]))
    wide_ref[...] = wide.reshape(128, table.shape[1]).astype(BF16)
    mask_ref[...] = jnp.where((iota((128, 1), 0) & 15) == owner, 1.0, 0.0).astype(BF16)

    def picks(size, index):
        return jnp.where(iota((size, width), 0) == index, 1.0, 0.0).astype(BF16)

    def body(i, carry):
        code = code_ref[pl.ds(i, 1), :]
        factor = dot(wide_ref[...], picks(wide_ref.shape[1], code & (CODE - 1)))
        factor = factor.astype(BF16) * mask_ref[...]
        matrix = lax.dot_general(
            factor,
            picks(parents, code >> 9),
            (((1,), (1,)), ((), ())),
            preferred_element_type=F32,
        )
        rows = pl.ds(pl.multiple_of(i * 16, 16), 16)
        matrix = matrix.reshape(8, 16, parents).astype(BF16)
        out_ref[:, rows, :] = matrix[:4]
        rest_ref[:, rows, :] = matrix[4:]
        return carry

    lax.fori_loop(0, blocks, body, 0, unroll=2)
    copy = pltpu.make_async_copy(rest_ref, rest_hbm, sem.at[0])
    copy.start()
    copy.wait()


def operators(far, trans, count, table):
    slots, parents = far.shape
    blocks = parents // 16
    return pl.pallas_call(
        operators_kernel,
        in_specs=[pl.BlockSpec(memory_space=pltpu.VMEM)] * 4,
        out_specs=[pl.BlockSpec(memory_space=pltpu.VMEM), pl.BlockSpec(memory_space=pltpu.HBM)],
        out_shape=[
            jax.ShapeDtypeStruct((4, parents, parents), BF16),
            pltpu.HBM((4, parents, parents), BF16),
        ],
        scratch_shapes=[
            pltpu.VMEM((blocks, 16 * slots), jnp.int32),
            pltpu.VMEM((128, table.shape[1]), BF16),
            pltpu.VMEM((128, 16 * slots), BF16),
            pltpu.VMEM((4, parents, parents), BF16),
            pltpu.SemaphoreType.DMA((1,)),
        ],
        compiler_params=pltpu.CompilerParams(vmem_limit_bytes=32 * MIB),
        cost_estimate=pl.CostEstimate(flops=12_000_000_000, bytes_accessed=3_000_000, transcendentals=0),
        name="operators",
    )(far, trans, count, table)


def translate_kernel(x_ref, m_ref, rest_hbm, out_ref, rest_ref, xp_ref, yp_ref, sem):
    groups = 4
    rows = x_ref.shape[0] // groups
    share = rows // 8
    owned = x_ref.shape[1] // 256
    parents = m_ref.shape[1]
    copy = pltpu.make_async_copy(rest_hbm, rest_ref, sem.at[0])
    copy.start()
    row, column = iota((rows, rows), 0), iota((rows, rows), 1)
    gather = jnp.where(column == (row & (share - 1)) * 8 + (row // share), 1.0, 0.0).astype(BF16)
    scatter = jnp.where(column == (row & 7) * share + (row >> 3), 1.0, 0.0).astype(BF16)
    for g in range(groups):
        xp_ref[g] = dot(gather, x_ref[g * rows : (g + 1) * rows, :]).astype(BF16)
    for j in range(4):
        if j == 2:
            copy.wait()
        from_ref = m_ref if j < 2 else rest_ref
        x = jnp.concatenate(
            [
                xp_ref[g, (c * 4 + j) * share : (c * 4 + j + 1) * share, p * 256 : (p + 1) * 256]
                for c in range(2)
                for p in range(owned)
                for g in range(groups)
            ],
            axis=0,
        )
        real, imag = from_ref[j % 2 * 2], from_ref[j % 2 * 2 + 1]
        y = dot(embedded(real, imag), x).astype(BF16)
        for c in range(2):
            for p in range(owned):
                for g in range(groups):
                    start = c * parents + (p * groups + g) * share
                    yp_ref[
                        g, (c * 4 + j) * share : (c * 4 + j + 1) * share, p * 256 : (p + 1) * 256
                    ] = y[start : start + share]
    for g in range(groups):
        out_ref[g * rows : (g + 1) * rows, :] = dot(scatter, yp_ref[g]).astype(BF16)


def translate(x, matrix, rest):
    rows, width = x.shape
    return pl.pallas_call(
        translate_kernel,
        in_specs=[pl.BlockSpec(memory_space=pltpu.VMEM)] * 2
        + [pl.BlockSpec(memory_space=pltpu.HBM)],
        out_specs=pl.BlockSpec(memory_space=pltpu.VMEM),
        out_shape=jax.ShapeDtypeStruct(x.shape, BF16),
        scratch_shapes=[
            pltpu.VMEM(rest.shape, BF16),
            pltpu.VMEM((4, rows // 4, width), BF16),
            pltpu.VMEM((4, rows // 4, width), BF16),
            pltpu.SemaphoreType.DMA((1,)),
        ],
        compiler_params=pltpu.CompilerParams(vmem_limit_bytes=32 * MIB),
        cost_estimate=pl.CostEstimate(flops=1_200_000_000, bytes_accessed=5_500_000, transcendentals=0),
        name="translate",
    )(x, matrix, pltpu.with_memory_space_constraint(rest, pltpu.HBM))


def near_kernel(index_ref, count_ref, low_ref, cur_ref, up_ref, tile_ref, out_ref, win_ref, sems):
    step = pl.program_id(0)
    group, slots = tile_ref.shape[:2]
    reach = low_ref.shape[1]
    boxes = cur_ref.shape[1]

    @pl.when(step == 0)
    def _():
        copies = []
        for c in range(2):
            rows = pl.ds(c * 128, 128)
            starts = ((low_ref, 0, reach), (cur_ref, reach, boxes), (up_ref, reach + boxes, reach))
            for n, (source, start, size) in enumerate(starts):
                copies.append(
                    pltpu.make_async_copy(
                        source.at[c], win_ref.at[pl.ds(start, size), rows, :], sems.at[c * 3 + n]
                    )
                )
        for copy in copies:
            copy.start()
        for copy in copies:
            copy.wait()

    @pl.loop(0, group)
    def _(i):
        box = step * group + i
        for live in range(1, slots + 1):

            @pl.when(count_ref[box] == live)
            def _():
                tiles = [embedded(tile_ref[i, s, 0], tile_ref[i, s, 1]) for s in range(live)]
                picked = [win_ref[index_ref[box * slots + s]] for s in range(live)]
                out_ref[i] = dot(
                    jnp.concatenate(tiles, axis=1), jnp.concatenate(picked, axis=0)
                ).astype(out_ref.dtype)


def near(index, count, low, currents, up, tiles):
    boxes, slots = tiles.shape[:2]
    reach = low.shape[1]
    group = 4
    return pl.pallas_call(
        near_kernel,
        grid_spec=pltpu.PrefetchScalarGridSpec(
            num_scalar_prefetch=2,
            grid=(boxes // group,),
            in_specs=[
                pl.BlockSpec(memory_space=pl.ANY),
                pl.BlockSpec(memory_space=pl.ANY),
                pl.BlockSpec(memory_space=pl.ANY),
                pl.BlockSpec((group, slots, 2, 128, 128), lambda b, i, n: (b, 0, 0, 0, 0)),
            ],
            out_specs=pl.BlockSpec((group, 256, 256), lambda b, i, n: (b, 0, 0)),
            scratch_shapes=[
                pltpu.VMEM((boxes + 2 * reach, 256, 256), BF16),
                pltpu.SemaphoreType.DMA((6,)),
            ],
        ),
        out_shape=pltpu.HBM((boxes, 256, 256), BF16),
        compiler_params=pltpu.CompilerParams(vmem_limit_bytes=60 * MIB),
        cost_estimate=pl.CostEstimate(flops=7_200_000_000, bytes_accessed=27_000_000, transcendentals=0),
        name="near",
    )(index, count, low, currents, up, tiles)


def downward_kernel(
    z_ref, interp_ref, angle_ref, rec_hbm, near_hbm, out_hbm,
    rec_ref, near_ref, w_ref, arr_ref, out_ref, in_sems, out_sems
):
    half = angle_ref.shape[1]
    parents = z_ref.shape[1] // 256
    coming = []
    for p in range(parents):
        of = pl.ds(p * 8, 8)
        coming.append(
            (
                pltpu.make_async_copy(rec_hbm.at[of], rec_ref.at[of], in_sems.at[p, 0]),
                pltpu.make_async_copy(near_hbm.at[of], near_ref.at[of], in_sems.at[p, 1]),
            )
        )
    for copy in coming[0]:
        copy.start()
    angle = angle_ref[...]
    cosine = jnp.cos(angle)
    sine = jnp.sin(angle)
    interp = interp_ref[...].astype(F32).T

    def matrix(c):
        ci = (cosine[c : c + 1] * interp).astype(BF16)
        si = (sine[c : c + 1] * interp).astype(BF16)
        w_ref[c * 256 : c * 256 + 128, :half] = ci
        w_ref[c * 256 : c * 256 + 128, half:] = si
        w_ref[c * 256 + 128 : c * 256 + 256, :half] = -si
        w_ref[c * 256 + 128 : c * 256 + 256, half:] = ci

    going = []
    for p in range(parents):
        z = separate(z_ref[:, p * 256 : (p + 1) * 256].astype(F32)).astype(BF16)
        pieces = 8
        for n in range(pieces):
            if p == 0:
                for c in range(n * 8 // pieces, (n + 1) * 8 // pieces):
                    matrix(c)
            rows = slice(n * 2048 // pieces, (n + 1) * 2048 // pieces)
            arr_ref[p % 2, rows, :] = dot(w_ref[rows, :], z).astype(BF16)
        for copy in coming[p]:
            copy.wait()
        if p + 1 < parents:
            for copy in coming[p + 1]:
                copy.start()
        for c in range(8):
            box = p * 8 + c
            arriving = arr_ref[p % 2, c * 256 : (c + 1) * 256, :]
            far = dot(embedded(rec_ref[box, 0], rec_ref[box, 1]), arriving)
            out_ref[:, box] = (far + near_ref[box].astype(F32)).astype(BF16).reshape(2, 128, 256)
            if c % 4 == 3:
                of = pl.ds(box - 3, 4)
                going.append(
                    pltpu.make_async_copy(
                        out_ref.at[:, of], out_hbm.at[:, of], out_sems.at[box // 4]
                    )
                )
                going[-1].start()
    for copy in going:
        copy.wait()


def downward(z, interp, angle, receive, near_field):
    boxes = receive.shape[0]
    response = (2, boxes, 128, 256)
    return pl.pallas_call(
        downward_kernel,
        in_specs=[pl.BlockSpec(memory_space=pltpu.VMEM)] * 3
        + [pl.BlockSpec(memory_space=pltpu.HBM)] * 2,
        out_specs=pl.BlockSpec(memory_space=pltpu.HBM),
        out_shape=jax.ShapeDtypeStruct(response, BF16),
        scratch_shapes=[
            pltpu.VMEM(receive.shape, BF16),
            pltpu.VMEM(near_field.shape, BF16),
            pltpu.VMEM((2048, 2 * interp.shape[0]), BF16),
            pltpu.VMEM((2, 2048, 256), BF16),
            pltpu.VMEM(response, BF16),
            pltpu.SemaphoreType.DMA((boxes // 8, 2)),
            pltpu.SemaphoreType.DMA((boxes // 4,)),
        ],
        compiler_params=pltpu.CompilerParams(vmem_limit_bytes=32 * MIB),
        cost_estimate=pl.CostEstimate(flops=5_000_000_000, bytes_accessed=13_000_000, transcendentals=0),
        name="downward",
    )(
        z,
        interp,
        angle,
        pltpu.with_memory_space_constraint(receive, pltpu.HBM),
        pltpu.with_memory_space_constraint(near_field, pltpu.HBM),
    )


def exchanged(value):
    return lax.all_to_all(value, AXES, split_axis=0, concat_axis=0, tiled=True)


def local(
    currents,
    near_tiles,
    near_index,
    near_count,
    radiate,
    receive,
    interp,
    shift_angle,
    far_index,
    far_count,
    trans_index,
    translators,
):
    boxes = currents.shape[1]
    reach = boxes // 2
    sent, leading, trailing = upward(currents, radiate, interp, shift_angle)
    by_direction = exchanged(sent)
    lower = passed_along(trailing, AXES, 1)
    upper = passed_along(leading, AXES, -1)

    table = translators.transpose(2, 1, 0).reshape(8, -1)
    table = jnp.pad(table, ((0, 0), (0, -table.shape[1] % 128)))
    matrix, rest = operators(far_index.T, trans_index.T, far_count[None, :], table)

    back = translate(by_direction, matrix, rest)
    incoming = exchanged(back)

    first = lax.axis_index(AXES) * boxes - reach
    near_field = near(
        (near_index - first).reshape(-1), near_count, lower, currents, upper, near_tiles
    )
    return downward(incoming, interp, shift_angle, receive, near_field)


def solution(mesh):
    placed = (
        P(None, AXES, None, None),
        P(AXES, None, None, None, None),
        P(AXES, None),
        P(AXES),
        P(AXES, None, None, None),
        P(AXES, None, None, None),
        P(),
        P(),
        P(),
        P(),
        P(),
        P(None, None, AXES),
    )
    return jax.shard_map(
        local,
        mesh=mesh,
        in_specs=placed,
        out_specs=P(None, AXES, None, None),
        check_vma=False,
    )
```

```python
import jax
import jax.numpy as jnp
from jax import lax
from jax.experimental import pallas as pl
from jax.experimental.pallas import tpu as pltpu
from jax.sharding import PartitionSpec as P

BF16 = jnp.bfloat16
F32 = jnp.float32
AXES = ("box", "dir")
MIB = 1 << 20
OWNED = 3
CODE = 512
DEAD = 1023


def passed_along(value, axis, by):
    peers = lax.axis_size(axis)
    pairs = [(i, i + by) for i in range(peers) if 0 <= i + by < peers]
    return lax.ppermute(value, axis, pairs)


def dot(left, right):
    return jnp.dot(left, right, preferred_element_type=F32)


def embedded(real, imag):
    return jnp.concatenate(
        [jnp.concatenate([real, -imag], axis=1), jnp.concatenate([imag, real], axis=1)], axis=0
    )


def interleave(upper, lower):
    rows, columns = upper.shape
    a = upper.reshape(rows // 8, 8, columns)
    b = lower.reshape(rows // 8, 8, columns)
    first = lax.broadcasted_iota(jnp.int32, a.shape, 1) < 4
    t = jnp.where(first, a, pltpu.roll(b, 4, 1))
    u = jnp.where(first, pltpu.roll(a, 4, 1), b)
    return jnp.stack([t, u], axis=1).reshape(2 * rows, columns)


def separate(mixed):
    rows, columns = mixed.shape
    parts = mixed.reshape(rows // 16, 2, 8, columns)
    t, u = parts[:, 0], parts[:, 1]
    first = lax.broadcasted_iota(jnp.int32, t.shape, 1) < 4
    a = jnp.where(first, t, pltpu.roll(u, 4, 1))
    b = jnp.where(first, pltpu.roll(t, 4, 1), u)
    return jnp.concatenate([a, b], axis=0).reshape(rows, columns)


def upward_kernel(
    cur_hbm, rad_hbm, interp_ref, angle_ref, out_hbm, first_hbm, last_hbm,
    cur_ref, rad_ref, w_ref, leaf_ref, out_ref, in_sems, halo_sems, out_sems
):
    half = interp_ref.shape[0]
    boxes = cur_ref.shape[1]
    parents = boxes // 8
    reach = first_hbm.shape[1]
    pieces = out_sems.shape[1]
    piece = half // pieces

    def arrivals(p):
        of = pl.ds(p * 8, 8)
        return (
            pltpu.make_async_copy(cur_hbm.at[:, of], cur_ref.at[:, of], in_sems.at[p, 0]),
            pltpu.make_async_copy(rad_hbm.at[of], rad_ref.at[of], in_sems.at[p, 1]),
        )

    for copy in arrivals(0):
        copy.start()

    angle = angle_ref[...]
    cosine = jnp.cos(angle).T
    sine = jnp.sin(angle).T
    interp = interp_ref[...].astype(F32)
    for c in range(8):
        ci = (cosine[:, c : c + 1] * interp).astype(BF16)
        si = (sine[:, c : c + 1] * interp).astype(BF16)
        left = slice(c * 256, c * 256 + 128)
        right = slice(c * 256 + 128, c * 256 + 256)
        for n in range(pieces):
            rows = slice(n * piece, (n + 1) * piece)
            real = slice(2 * n * piece, (2 * n + 1) * piece)
            imag = slice((2 * n + 1) * piece, (2 * n + 2) * piece)
            w_ref[real, left] = ci[rows]
            w_ref[real, right] = -si[rows]
            w_ref[imag, left] = si[rows]
            w_ref[imag, right] = ci[rows]

    def departures(p):
        lanes = pl.ds(pl.multiple_of(p * 256, 256), 256)
        copies = []
        for n in range(pieces):
            rows = pl.ds(2 * n * piece, 2 * piece)
            copies.append(
                pltpu.make_async_copy(
                    out_ref.at[p, rows], out_hbm.at[rows, lanes], out_sems.at[p, n]
                )
            )
        return copies

    halos = []
    for n, (start, target) in enumerate(((0, first_hbm), (boxes - reach, last_hbm))):
        source = cur_ref.at[:, pl.ds(start, reach)]
        halos.append(pltpu.make_async_copy(source, target, halo_sems.at[n]))

    def body(p, carry):
        for copy in arrivals(p):
            copy.wait()

        @pl.when(p + 1 < parents)
        def _():
            for copy in arrivals(p + 1):
                copy.start()

        @pl.when(p + 1 == parents)
        def _():
            for copy in halos:
                copy.start()

        for c in range(8):
            box = p * 8 + c
            x = cur_ref[:, box].reshape(256, 256)
            leaf = dot(embedded(rad_ref[box, 0], rad_ref[box, 1]), x)
            leaf_ref[c * 256 : (c + 1) * 256, :] = leaf.astype(BF16)
        for n, copy in enumerate(departures(p)):
            rows = slice(2 * n * piece, (2 * n + 2) * piece)
            y = dot(w_ref[rows], leaf_ref[...])
            out_ref[p, rows, :] = interleave(y[:piece], y[piece:]).astype(BF16)
            copy.start()
        return carry

    lax.fori_loop(0, parents, body, 0)
    for p in range(parents):
        for copy in departures(p):
            copy.wait()
    for copy in halos:
        copy.wait()


def upward(currents, radiate, interp, angle):
    parts, boxes, unknowns, columns = currents.shape
    parents = boxes // 8
    directions = interp.shape[0]
    sent = (2 * directions, parents * columns)
    halo = jax.ShapeDtypeStruct((parts, boxes // 2, unknowns, columns), BF16)
    return pl.pallas_call(
        upward_kernel,
        in_specs=[
            pl.BlockSpec(memory_space=pltpu.HBM),
            pl.BlockSpec(memory_space=pltpu.HBM),
            pl.BlockSpec(memory_space=pltpu.VMEM),
            pl.BlockSpec(memory_space=pltpu.VMEM),
        ],
        out_specs=[pl.BlockSpec(memory_space=pl.ANY)] * 3,
        out_shape=[jax.ShapeDtypeStruct(sent, BF16), halo, halo],
        scratch_shapes=[
            pltpu.VMEM(currents.shape, BF16),
            pltpu.VMEM(radiate.shape, BF16),
            pltpu.VMEM((2 * directions, 2048), BF16),
            pltpu.VMEM((2048, 256), BF16),
            pltpu.VMEM((parents, 2 * directions, columns), BF16),
            pltpu.SemaphoreType.DMA((parents, 2)),
            pltpu.SemaphoreType.DMA((2,)),
            pltpu.SemaphoreType.DMA((parents, 2)),
        ],
        compiler_params=pltpu.CompilerParams(vmem_limit_bytes=60 * MIB),
        cost_estimate=pl.CostEstimate(flops=5_000_000_000, bytes_accessed=7_000_000, transcendentals=0),
        name="upward",
    )(currents, radiate, interp, angle)


def iota(shape, axis):
    return lax.broadcasted_iota(jnp.int32, shape, axis)


def operators_kernel(
    far_ref, trans_ref, count_ref, table_ref, out_ref, rest_hbm, code_ref, wide_ref, mask_ref, rest_ref, sem
):
    slots, parents = far_ref.shape
    blocks, width = code_ref.shape
    owned = OWNED
    devices = parents // owned
    per = blocks // owned

    def device(p):
        return (p * (65536 // owned + 1)) >> 16

    far = far_ref[...]
    source = (far - device(far) * owned) * devices + device(far)
    live = iota(far.shape, 0) < count_ref[...]
    code = jnp.where(live, source, DEAD) * CODE + trans_ref[...]
    lane = iota((1, width), 1)
    owner = lane // slots
    spread = jnp.where(iota((slots, width), 0) == lane - owner * slots, 1.0, 0.0)
    exact = dict(precision=lax.Precision.HIGHEST, preferred_element_type=F32)
    flat = jnp.dot(code.astype(F32).T, spread, **exact)
    flat = jnp.where((device(iota((parents, 1), 0)) & 15) == owner, flat, 0.0)
    p = iota((1, parents), 1)
    block = (p - device(p) * owned) * per + (device(p) >> 4)
    member = jnp.where(iota((blocks, parents), 0) == block, 1.0, 0.0)
    code_ref[...] = jnp.dot(member, flat, **exact).astype(jnp.int32)
    table = table_ref[...]
    wide = jnp.broadcast_to(table[:, None, :], (8, 16, table.shape[1]))
    wide_ref[...] = wide.reshape(128, table.shape[1]).astype(BF16)
    mask_ref[...] = jnp.where((iota((128, 1), 0) & 15) == owner, 1.0, 0.0).astype(BF16)

    def picks(size, index):
        return jnp.where(iota((size, width), 0) == index, 1.0, 0.0).astype(BF16)

    def body(i, carry):
        code = code_ref[pl.ds(i, 1), :]
        factor = dot(wide_ref[...], picks(wide_ref.shape[1], code & (CODE - 1)))
        factor = factor.astype(BF16) * mask_ref[...]
        matrix = lax.dot_general(
            factor,
            picks(parents, code >> 9),
            (((1,), (1,)), ((), ())),
            preferred_element_type=F32,
        )
        rows = pl.ds(pl.multiple_of(i * 16, 16), 16)
        matrix = matrix.reshape(8, 16, parents).astype(BF16)
        out_ref[:, rows, :] = matrix[:4]
        rest_ref[:, rows, :] = matrix[4:]
        return carry

    lax.fori_loop(0, blocks, body, 0, unroll=2)
    copy = pltpu.make_async_copy(rest_ref, rest_hbm, sem.at[0])
    copy.start()
    copy.wait()


def operators(far, trans, count, table):
    slots, parents = far.shape
    blocks = parents // 16
    return pl.pallas_call(
        operators_kernel,
        in_specs=[pl.BlockSpec(memory_space=pltpu.VMEM)] * 4,
        out_specs=[pl.BlockSpec(memory_space=pltpu.VMEM), pl.BlockSpec(memory_space=pltpu.HBM)],
        out_shape=[
            jax.ShapeDtypeStruct((4, parents, parents), BF16),
            pltpu.HBM((4, parents, parents), BF16),
        ],
        scratch_shapes=[
            pltpu.VMEM((blocks, 16 * slots), jnp.int32),
            pltpu.VMEM((128, table.shape[1]), BF16),
            pltpu.VMEM((128, 16 * slots), BF16),
            pltpu.VMEM((4, parents, parents), BF16),
            pltpu.SemaphoreType.DMA((1,)),
        ],
        compiler_params=pltpu.CompilerParams(vmem_limit_bytes=32 * MIB),
        cost_estimate=pl.CostEstimate(flops=12_000_000_000, bytes_accessed=3_000_000, transcendentals=0),
        name="operators",
    )(far, trans, count, table)


def translate_kernel(x_ref, m_ref, rest_hbm, out_hbm, rest_ref, xp_ref, yp_ref, out_ref, sem, out_sems):
    groups = 4
    rows = x_ref.shape[0] // groups
    share = rows // 8
    owned = x_ref.shape[1] // 256
    parents = m_ref.shape[1]
    copy = pltpu.make_async_copy(rest_hbm, rest_ref, sem.at[0])
    copy.start()
    row, column = iota((rows, rows), 0), iota((rows, rows), 1)
    gather = jnp.where(column == (row & (share - 1)) * 8 + (row // share), 1.0, 0.0).astype(BF16)
    scatter = jnp.where(column == (row & 7) * share + (row >> 3), 1.0, 0.0).astype(BF16)
    for g in range(groups):
        xp_ref[g] = dot(gather, x_ref[g * rows : (g + 1) * rows, :]).astype(BF16)
    for j in range(4):
        if j == 2:
            copy.wait()
        from_ref = m_ref if j < 2 else rest_ref
        x = jnp.concatenate(
            [
                xp_ref[g, (c * 4 + j) * share : (c * 4 + j + 1) * share, p * 256 : (p + 1) * 256]
                for c in range(2)
                for p in range(owned)
                for g in range(groups)
            ],
            axis=0,
        )
        real, imag = from_ref[j % 2 * 2], from_ref[j % 2 * 2 + 1]
        y = dot(embedded(real, imag), x).astype(BF16)
        for c in range(2):
            for p in range(owned):
                for g in range(groups):
                    start = c * parents + (p * groups + g) * share
                    yp_ref[
                        g, (c * 4 + j) * share : (c * 4 + j + 1) * share, p * 256 : (p + 1) * 256
                    ] = y[start : start + share]
    going = []
    for g in range(groups):
        out_ref[g * rows : (g + 1) * rows, :] = dot(scatter, yp_ref[g]).astype(BF16)
        of = pl.ds(g * rows, rows)
        going.append(pltpu.make_async_copy(out_ref.at[of], out_hbm.at[of], out_sems.at[g]))
        going[-1].start()
    for copy in going:
        copy.wait()


def translate(x, matrix, rest):
    rows, width = x.shape
    return pl.pallas_call(
        translate_kernel,
        in_specs=[pl.BlockSpec(memory_space=pltpu.VMEM)] * 2
        + [pl.BlockSpec(memory_space=pltpu.HBM)],
        out_specs=pl.BlockSpec(memory_space=pltpu.HBM),
        out_shape=pltpu.HBM(x.shape, BF16),
        scratch_shapes=[
            pltpu.VMEM(rest.shape, BF16),
            pltpu.VMEM((4, rows // 4, width), BF16),
            pltpu.VMEM((4, rows // 4, width), BF16),
            pltpu.VMEM(x.shape, BF16),
            pltpu.SemaphoreType.DMA((1,)),
            pltpu.SemaphoreType.DMA((4,)),
        ],
        compiler_params=pltpu.CompilerParams(vmem_limit_bytes=32 * MIB),
        cost_estimate=pl.CostEstimate(flops=1_200_000_000, bytes_accessed=5_500_000, transcendentals=0),
        name="translate",
    )(x, matrix, pltpu.with_memory_space_constraint(rest, pltpu.HBM))


def near_kernel(index_ref, count_ref, low_ref, cur_ref, up_ref, tile_ref, out_ref, win_ref, sems):
    step = pl.program_id(0)
    group, slots = tile_ref.shape[:2]
    reach = low_ref.shape[1]
    boxes = cur_ref.shape[1]

    @pl.when(step == 0)
    def _():
        copies = []
        for c in range(2):
            rows = pl.ds(c * 128, 128)
            starts = ((low_ref, 0, reach), (cur_ref, reach, boxes), (up_ref, reach + boxes, reach))
            for n, (source, start, size) in enumerate(starts):
                copies.append(
                    pltpu.make_async_copy(
                        source.at[c], win_ref.at[pl.ds(start, size), rows, :], sems.at[c * 3 + n]
                    )
                )
        for copy in copies:
            copy.start()
        for copy in copies:
            copy.wait()

    @pl.loop(0, group)
    def _(i):
        box = step * group + i
        for live in range(1, slots + 1):

            @pl.when(count_ref[box] == live)
            def _():
                tiles = [embedded(tile_ref[i, s, 0], tile_ref[i, s, 1]) for s in range(live)]
                picked = [win_ref[index_ref[box * slots + s]] for s in range(live)]
                out_ref[i] = dot(
                    jnp.concatenate(tiles, axis=1), jnp.concatenate(picked, axis=0)
                ).astype(out_ref.dtype)


def near(index, count, low, currents, up, tiles):
    boxes, slots = tiles.shape[:2]
    reach = low.shape[1]
    group = 4
    return pl.pallas_call(
        near_kernel,
        grid_spec=pltpu.PrefetchScalarGridSpec(
            num_scalar_prefetch=2,
            grid=(boxes // group,),
            in_specs=[
                pl.BlockSpec(memory_space=pl.ANY),
                pl.BlockSpec(memory_space=pl.ANY),
                pl.BlockSpec(memory_space=pl.ANY),
                pl.BlockSpec((group, slots, 2, 128, 128), lambda b, i, n: (b, 0, 0, 0, 0)),
            ],
            out_specs=pl.BlockSpec((group, 256, 256), lambda b, i, n: (b, 0, 0)),
            scratch_shapes=[
                pltpu.VMEM((boxes + 2 * reach, 256, 256), BF16),
                pltpu.SemaphoreType.DMA((6,)),
            ],
        ),
        out_shape=pltpu.HBM((boxes, 256, 256), BF16),
        compiler_params=pltpu.CompilerParams(vmem_limit_bytes=60 * MIB),
        cost_estimate=pl.CostEstimate(flops=7_200_000_000, bytes_accessed=27_000_000, transcendentals=0),
        name="near",
    )(index, count, low, currents, up, tiles)


def downward_kernel(
    z_ref, interp_ref, angle_ref, rec_hbm, near_hbm, out_hbm,
    rec_ref, near_ref, w_ref, arr_ref, out_ref, in_sems, out_sems
):
    half = angle_ref.shape[1]
    parents = z_ref.shape[1] // 256
    coming = []
    for p in range(parents):
        of = pl.ds(p * 8, 8)
        coming.append(
            (
                pltpu.make_async_copy(rec_hbm.at[of], rec_ref.at[of], in_sems.at[p, 0]),
                pltpu.make_async_copy(near_hbm.at[of], near_ref.at[of], in_sems.at[p, 1]),
            )
        )
    for copy in coming[0]:
        copy.start()
    angle = angle_ref[...]
    cosine = jnp.cos(angle)
    sine = jnp.sin(angle)
    interp = interp_ref[...].astype(F32).T

    def matrix(c):
        ci = (cosine[c : c + 1] * interp).astype(BF16)
        si = (sine[c : c + 1] * interp).astype(BF16)
        w_ref[c * 256 : c * 256 + 128, :half] = ci
        w_ref[c * 256 : c * 256 + 128, half:] = si
        w_ref[c * 256 + 128 : c * 256 + 256, :half] = -si
        w_ref[c * 256 + 128 : c * 256 + 256, half:] = ci

    going = []
    for p in range(parents):
        z = separate(z_ref[:, p * 256 : (p + 1) * 256].astype(F32)).astype(BF16)
        pieces = 8
        for n in range(pieces):
            if p == 0:
                for c in range(n * 8 // pieces, (n + 1) * 8 // pieces):
                    matrix(c)
            rows = slice(n * 2048 // pieces, (n + 1) * 2048 // pieces)
            arr_ref[p % 2, rows, :] = dot(w_ref[rows, :], z).astype(BF16)
        for copy in coming[p]:
            copy.wait()
        if p + 1 < parents:
            for copy in coming[p + 1]:
                copy.start()
        for c in range(8):
            box = p * 8 + c
            arriving = arr_ref[p % 2, c * 256 : (c + 1) * 256, :]
            far = dot(embedded(rec_ref[box, 0], rec_ref[box, 1]), arriving)
            out_ref[:, box] = (far + near_ref[box].astype(F32)).astype(BF16).reshape(2, 128, 256)
            if c % 4 == 3:
                of = pl.ds(box - 3, 4)
                going.append(
                    pltpu.make_async_copy(
                        out_ref.at[:, of], out_hbm.at[:, of], out_sems.at[box // 4]
                    )
                )
                going[-1].start()
    for copy in going:
        copy.wait()


def downward(z, interp, angle, receive, near_field):
    boxes = receive.shape[0]
    response = (2, boxes, 128, 256)
    return pl.pallas_call(
        downward_kernel,
        in_specs=[pl.BlockSpec(memory_space=pltpu.VMEM)] * 3
        + [pl.BlockSpec(memory_space=pltpu.HBM)] * 2,
        out_specs=pl.BlockSpec(memory_space=pltpu.HBM),
        out_shape=jax.ShapeDtypeStruct(response, BF16),
        scratch_shapes=[
            pltpu.VMEM(receive.shape, BF16),
            pltpu.VMEM(near_field.shape, BF16),
            pltpu.VMEM((2048, 2 * interp.shape[0]), BF16),
            pltpu.VMEM((2, 2048, 256), BF16),
            pltpu.VMEM(response, BF16),
            pltpu.SemaphoreType.DMA((boxes // 8, 2)),
            pltpu.SemaphoreType.DMA((boxes // 4,)),
        ],
        compiler_params=pltpu.CompilerParams(vmem_limit_bytes=32 * MIB),
        cost_estimate=pl.CostEstimate(flops=5_000_000_000, bytes_accessed=13_000_000, transcendentals=0),
        name="downward",
    )(
        z,
        interp,
        angle,
        pltpu.with_memory_space_constraint(receive, pltpu.HBM),
        pltpu.with_memory_space_constraint(near_field, pltpu.HBM),
    )


def exchanged(value):
    return lax.all_to_all(value, AXES, split_axis=0, concat_axis=0, tiled=True)


def local(
    currents,
    near_tiles,
    near_index,
    near_count,
    radiate,
    receive,
    interp,
    shift_angle,
    far_index,
    far_count,
    trans_index,
    translators,
):
    boxes = currents.shape[1]
    reach = boxes // 2
    sent, leading, trailing = upward(currents, radiate, interp, shift_angle)
    by_direction = exchanged(sent)
    lower = passed_along(trailing, AXES, 1)
    upper = passed_along(leading, AXES, -1)

    table = translators.transpose(2, 1, 0).reshape(8, -1)
    table = jnp.pad(table, ((0, 0), (0, -table.shape[1] % 128)))
    matrix, rest = operators(far_index.T, trans_index.T, far_count[None, :], table)

    back = translate(by_direction, matrix, rest)
    incoming = exchanged(back)

    first = lax.axis_index(AXES) * boxes - reach
    near_field = near(
        (near_index - first).reshape(-1), near_count, lower, currents, upper, near_tiles
    )
    return downward(incoming, interp, shift_angle, receive, near_field)


def solution(mesh):
    placed = (
        P(None, AXES, None, None),
        P(AXES, None, None, None, None),
        P(AXES, None),
        P(AXES),
        P(AXES, None, None, None),
        P(AXES, None, None, None),
        P(),
        P(),
        P(),
        P(),
        P(),
        P(None, None, AXES),
    )
    return jax.shard_map(
        local,
        mesh=mesh,
        in_specs=placed,
        out_specs=P(None, AXES, None, None),
        check_vma=False,
    )
```

```python
import jax
import jax.numpy as jnp
from jax import lax
from jax.experimental import pallas as pl
from jax.experimental.pallas import tpu as pltpu
from jax.sharding import PartitionSpec as P

BF16 = jnp.bfloat16
F32 = jnp.float32
AXES = ("box", "dir")
MIB = 1 << 20
OWNED = 3
CODE = 512
DEAD = 1023


def passed_along(value, axis, by):
    peers = lax.axis_size(axis)
    pairs = [(i, i + by) for i in range(peers) if 0 <= i + by < peers]
    return lax.ppermute(value, axis, pairs)


def dot(left, right):
    return jnp.dot(left, right, preferred_element_type=F32)


def embedded(real, imag):
    return jnp.concatenate(
        [jnp.concatenate([real, -imag], axis=1), jnp.concatenate([imag, real], axis=1)], axis=0
    )


def interleave(upper, lower):
    rows, columns = upper.shape
    a = upper.reshape(rows // 8, 8, columns)
    b = lower.reshape(rows // 8, 8, columns)
    first = lax.broadcasted_iota(jnp.int32, a.shape, 1) < 4
    t = jnp.where(first, a, pltpu.roll(b, 4, 1))
    u = jnp.where(first, pltpu.roll(a, 4, 1), b)
    return jnp.stack([t, u], axis=1).reshape(2 * rows, columns)


def separate(mixed):
    rows, columns = mixed.shape
    parts = mixed.reshape(rows // 16, 2, 8, columns)
    t, u = parts[:, 0], parts[:, 1]
    first = lax.broadcasted_iota(jnp.int32, t.shape, 1) < 4
    a = jnp.where(first, t, pltpu.roll(u, 4, 1))
    b = jnp.where(first, pltpu.roll(t, 4, 1), u)
    return jnp.concatenate([a, b], axis=0).reshape(rows, columns)


def upward_kernel(
    cur_hbm, rad_hbm, interp_ref, angle_ref, out_hbm, first_hbm, last_hbm,
    cur_ref, rad_ref, w_ref, leaf_ref, out_ref, in_sems, halo_sems, out_sems
):
    half = interp_ref.shape[0]
    boxes = cur_ref.shape[1]
    parents = boxes // 8
    reach = first_hbm.shape[1]
    pieces = out_sems.shape[1]
    piece = half // pieces

    def arrivals(p):
        of = pl.ds(p * 8, 8)
        return (
            pltpu.make_async_copy(cur_hbm.at[:, of], cur_ref.at[:, of], in_sems.at[p, 0]),
            pltpu.make_async_copy(rad_hbm.at[of], rad_ref.at[of], in_sems.at[p, 1]),
        )

    for copy in arrivals(0):
        copy.start()

    angle = angle_ref[...]
    cosine = jnp.cos(angle).T
    sine = jnp.sin(angle).T
    interp = interp_ref[...].astype(F32)
    for c in range(8):
        ci = (cosine[:, c : c + 1] * interp).astype(BF16)
        si = (sine[:, c : c + 1] * interp).astype(BF16)
        left = slice(c * 256, c * 256 + 128)
        right = slice(c * 256 + 128, c * 256 + 256)
        for n in range(pieces):
            rows = slice(n * piece, (n + 1) * piece)
            real = slice(2 * n * piece, (2 * n + 1) * piece)
            imag = slice((2 * n + 1) * piece, (2 * n + 2) * piece)
            w_ref[real, left] = ci[rows]
            w_ref[real, right] = -si[rows]
            w_ref[imag, left] = si[rows]
            w_ref[imag, right] = ci[rows]

    def departures(p):
        lanes = pl.ds(pl.multiple_of(p * 256, 256), 256)
        copies = []
        for n in range(pieces):
            rows = pl.ds(2 * n * piece, 2 * piece)
            copies.append(
                pltpu.make_async_copy(
                    out_ref.at[p, rows], out_hbm.at[rows, lanes], out_sems.at[p, n]
                )
            )
        return copies

    halos = []
    for n, (start, target) in enumerate(((0, first_hbm), (boxes - reach, last_hbm))):
        source = cur_ref.at[:, pl.ds(start, reach)]
        halos.append(pltpu.make_async_copy(source, target, halo_sems.at[n]))

    def body(p, carry):
        for copy in arrivals(p):
            copy.wait()

        @pl.when(p + 1 < parents)
        def _():
            for copy in arrivals(p + 1):
                copy.start()

        @pl.when(p + 1 == parents)
        def _():
            for copy in halos:
                copy.start()

        for c in range(8):
            box = p * 8 + c
            x = cur_ref[:, box].reshape(256, 256)
            leaf = dot(embedded(rad_ref[box, 0], rad_ref[box, 1]), x)
            leaf_ref[c * 256 : (c + 1) * 256, :] = leaf.astype(BF16)
        for n, copy in enumerate(departures(p)):
            rows = slice(2 * n * piece, (2 * n + 2) * piece)
            y = dot(w_ref[rows], leaf_ref[...])
            out_ref[p, rows, :] = interleave(y[:piece], y[piece:]).astype(BF16)
            copy.start()
        return carry

    lax.fori_loop(0, parents, body, 0)
    for p in range(parents):
        for copy in departures(p):
            copy.wait()
    for copy in halos:
        copy.wait()


def upward(currents, radiate, interp, angle):
    parts, boxes, unknowns, columns = currents.shape
    parents = boxes // 8
    directions = interp.shape[0]
    sent = (2 * directions, parents * columns)
    halo = jax.ShapeDtypeStruct((parts, boxes // 2, unknowns, columns), BF16)
    return pl.pallas_call(
        upward_kernel,
        in_specs=[
            pl.BlockSpec(memory_space=pltpu.HBM),
            pl.BlockSpec(memory_space=pltpu.HBM),
            pl.BlockSpec(memory_space=pltpu.VMEM),
            pl.BlockSpec(memory_space=pltpu.VMEM),
        ],
        out_specs=[pl.BlockSpec(memory_space=pl.ANY)] * 3,
        out_shape=[jax.ShapeDtypeStruct(sent, BF16), halo, halo],
        scratch_shapes=[
            pltpu.VMEM(currents.shape, BF16),
            pltpu.VMEM(radiate.shape, BF16),
            pltpu.VMEM((2 * directions, 2048), BF16),
            pltpu.VMEM((2048, 256), BF16),
            pltpu.VMEM((parents, 2 * directions, columns), BF16),
            pltpu.SemaphoreType.DMA((parents, 4)),
            pltpu.SemaphoreType.DMA((2,)),
            pltpu.SemaphoreType.DMA((parents, 4)),
        ],
        compiler_params=pltpu.CompilerParams(vmem_limit_bytes=60 * MIB),
        cost_estimate=pl.CostEstimate(flops=5_000_000_000, bytes_accessed=7_000_000, transcendentals=0),
        name="upward",
    )(currents, radiate, interp, angle)


def iota(shape, axis):
    return lax.broadcasted_iota(jnp.int32, shape, axis)


def operators_kernel(
    far_ref, trans_ref, count_ref, table_ref, out_ref, rest_hbm, code_ref, wide_ref, mask_ref, rest_ref, sem
):
    slots, parents = far_ref.shape
    blocks, width = code_ref.shape
    owned = OWNED
    devices = parents // owned
    per = blocks // owned

    def device(p):
        return (p * (65536 // owned + 1)) >> 16

    far = far_ref[...]
    source = (far - device(far) * owned) * devices + device(far)
    live = iota(far.shape, 0) < count_ref[...]
    code = jnp.where(live, source, DEAD) * CODE + trans_ref[...]
    lane = iota((1, width), 1)
    owner = lane // slots
    spread = jnp.where(iota((slots, width), 0) == lane - owner * slots, 1.0, 0.0)
    exact = dict(precision=lax.Precision.HIGHEST, preferred_element_type=F32)
    flat = jnp.dot(code.astype(F32).T, spread, **exact)
    flat = jnp.where((device(iota((parents, 1), 0)) & 15) == owner, flat, 0.0)
    p = iota((1, parents), 1)
    block = (p - device(p) * owned) * per + (device(p) >> 4)
    member = jnp.where(iota((blocks, parents), 0) == block, 1.0, 0.0)
    code_ref[...] = jnp.dot(member, flat, **exact).astype(jnp.int32)
    table = table_ref[...]
    wide = jnp.broadcast_to(table[:, None, :], (8, 16, table.shape[1]))
    wide_ref[...] = wide.reshape(128, table.shape[1]).astype(BF16)
    mask_ref[...] = jnp.where((iota((128, 1), 0) & 15) == owner, 1.0, 0.0).astype(BF16)

    def picks(size, index):
        return jnp.where(iota((size, width), 0) == index, 1.0, 0.0).astype(BF16)

    def body(i, carry):
        code = code_ref[pl.ds(i, 1), :]
        factor = dot(wide_ref[...], picks(wide_ref.shape[1], code & (CODE - 1)))
        factor = factor.astype(BF16) * mask_ref[...]
        matrix = lax.dot_general(
            factor,
            picks(parents, code >> 9),
            (((1,), (1,)), ((), ())),
            preferred_element_type=F32,
        )
        rows = pl.ds(pl.multiple_of(i * 16, 16), 16)
        matrix = matrix.reshape(8, 16, parents).astype(BF16)
        out_ref[:, rows, :] = matrix[:4]
        rest_ref[:, rows, :] = matrix[4:]
        return carry

    lax.fori_loop(0, blocks, body, 0, unroll=4)
    copy = pltpu.make_async_copy(rest_ref, rest_hbm, sem.at[0])
    copy.start()
    copy.wait()


def operators(far, trans, count, table):
    slots, parents = far.shape
    blocks = parents // 16
    return pl.pallas_call(
        operators_kernel,
        in_specs=[pl.BlockSpec(memory_space=pltpu.VMEM)] * 4,
        out_specs=[pl.BlockSpec(memory_space=pltpu.VMEM), pl.BlockSpec(memory_space=pltpu.HBM)],
        out_shape=[
            jax.ShapeDtypeStruct((4, parents, parents), BF16),
            pltpu.HBM((4, parents, parents), BF16),
        ],
        scratch_shapes=[
            pltpu.VMEM((blocks, 16 * slots), jnp.int32),
            pltpu.VMEM((128, table.shape[1]), BF16),
            pltpu.VMEM((128, 16 * slots), BF16),
            pltpu.VMEM((4, parents, parents), BF16),
            pltpu.SemaphoreType.DMA((1,)),
        ],
        compiler_params=pltpu.CompilerParams(vmem_limit_bytes=32 * MIB),
        cost_estimate=pl.CostEstimate(flops=12_000_000_000, bytes_accessed=3_000_000, transcendentals=0),
        name="operators",
    )(far, trans, count, table)


def translate_kernel(x_ref, m_ref, rest_hbm, out_hbm, rest_ref, xp_ref, yp_ref, out_ref, sem, out_sems):
    groups = 4
    rows = x_ref.shape[0] // groups
    share = rows // 8
    owned = x_ref.shape[1] // 256
    parents = m_ref.shape[1]
    copy = pltpu.make_async_copy(rest_hbm, rest_ref, sem.at[0])
    copy.start()
    row, column = iota((rows, rows), 0), iota((rows, rows), 1)
    gather = jnp.where(column == (row & (share - 1)) * 8 + (row // share), 1.0, 0.0).astype(BF16)
    scatter = jnp.where(column == (row & 7) * share + (row >> 3), 1.0, 0.0).astype(BF16)
    for g in range(groups):
        xp_ref[g] = dot(gather, x_ref[g * rows : (g + 1) * rows, :]).astype(BF16)
    for j in range(4):
        if j == 2:
            copy.wait()
        from_ref = m_ref if j < 2 else rest_ref
        x = jnp.concatenate(
            [
                xp_ref[g, (c * 4 + j) * share : (c * 4 + j + 1) * share, p * 256 : (p + 1) * 256]
                for c in range(2)
                for p in range(owned)
                for g in range(groups)
            ],
            axis=0,
        )
        real, imag = from_ref[j % 2 * 2], from_ref[j % 2 * 2 + 1]
        y = dot(embedded(real, imag), x).astype(BF16)
        for c in range(2):
            for p in range(owned):
                for g in range(groups):
                    start = c * parents + (p * groups + g) * share
                    yp_ref[
                        g, (c * 4 + j) * share : (c * 4 + j + 1) * share, p * 256 : (p + 1) * 256
                    ] = y[start : start + share]
    going = []
    for g in range(groups):
        out_ref[g * rows : (g + 1) * rows, :] = dot(scatter, yp_ref[g]).astype(BF16)
        of = pl.ds(g * rows, rows)
        going.append(pltpu.make_async_copy(out_ref.at[of], out_hbm.at[of], out_sems.at[g]))
        going[-1].start()
    for copy in going:
        copy.wait()


def translate(x, matrix, rest):
    rows, width = x.shape
    return pl.pallas_call(
        translate_kernel,
        in_specs=[pl.BlockSpec(memory_space=pltpu.VMEM)] * 2
        + [pl.BlockSpec(memory_space=pltpu.HBM)],
        out_specs=pl.BlockSpec(memory_space=pltpu.HBM),
        out_shape=pltpu.HBM(x.shape, BF16),
        scratch_shapes=[
            pltpu.VMEM(rest.shape, BF16),
            pltpu.VMEM((4, rows // 4, width), BF16),
            pltpu.VMEM((4, rows // 4, width), BF16),
            pltpu.VMEM(x.shape, BF16),
            pltpu.SemaphoreType.DMA((1,)),
            pltpu.SemaphoreType.DMA((4,)),
        ],
        compiler_params=pltpu.CompilerParams(vmem_limit_bytes=32 * MIB),
        cost_estimate=pl.CostEstimate(flops=1_200_000_000, bytes_accessed=5_500_000, transcendentals=0),
        name="translate",
    )(x, matrix, pltpu.with_memory_space_constraint(rest, pltpu.HBM))


def near_kernel(index_ref, count_ref, low_ref, cur_ref, up_ref, tile_ref, out_ref, win_ref, sems):
    step = pl.program_id(0)
    group, slots = tile_ref.shape[:2]
    reach = low_ref.shape[1]
    boxes = cur_ref.shape[1]

    @pl.when(step == 0)
    def _():
        copies = []
        for c in range(2):
            rows = pl.ds(c * 128, 128)
            starts = ((low_ref, 0, reach), (cur_ref, reach, boxes), (up_ref, reach + boxes, reach))
            for n, (source, start, size) in enumerate(starts):
                copies.append(
                    pltpu.make_async_copy(
                        source.at[c], win_ref.at[pl.ds(start, size), rows, :], sems.at[c * 3 + n]
                    )
                )
        for copy in copies:
            copy.start()
        for copy in copies:
            copy.wait()

    @pl.loop(0, group)
    def _(i):
        box = step * group + i
        for live in range(1, slots + 1):

            @pl.when(count_ref[box] == live)
            def _():
                tiles = [embedded(tile_ref[i, s, 0], tile_ref[i, s, 1]) for s in range(live)]
                picked = [win_ref[index_ref[box * slots + s]] for s in range(live)]
                out_ref[i] = dot(
                    jnp.concatenate(tiles, axis=1), jnp.concatenate(picked, axis=0)
                ).astype(out_ref.dtype)


def near(index, count, low, currents, up, tiles):
    boxes, slots = tiles.shape[:2]
    reach = low.shape[1]
    group = 4
    return pl.pallas_call(
        near_kernel,
        grid_spec=pltpu.PrefetchScalarGridSpec(
            num_scalar_prefetch=2,
            grid=(boxes // group,),
            in_specs=[
                pl.BlockSpec(memory_space=pl.ANY),
                pl.BlockSpec(memory_space=pl.ANY),
                pl.BlockSpec(memory_space=pl.ANY),
                pl.BlockSpec((group, slots, 2, 128, 128), lambda b, i, n: (b, 0, 0, 0, 0)),
            ],
            out_specs=pl.BlockSpec((group, 256, 256), lambda b, i, n: (b, 0, 0)),
            scratch_shapes=[
                pltpu.VMEM((boxes + 2 * reach, 256, 256), BF16),
                pltpu.SemaphoreType.DMA((6,)),
            ],
        ),
        out_shape=pltpu.HBM((boxes, 256, 256), BF16),
        compiler_params=pltpu.CompilerParams(vmem_limit_bytes=60 * MIB),
        cost_estimate=pl.CostEstimate(flops=7_200_000_000, bytes_accessed=27_000_000, transcendentals=0),
        name="near",
    )(index, count, low, currents, up, tiles)


def downward_kernel(
    z_ref, interp_ref, angle_ref, rec_hbm, near_hbm, out_hbm,
    rec_ref, near_ref, w_ref, arr_ref, out_ref, in_sems, out_sems
):
    half = angle_ref.shape[1]
    parents = z_ref.shape[1] // 256
    coming = []
    for p in range(parents):
        of = pl.ds(p * 8, 8)
        coming.append(
            (
                pltpu.make_async_copy(rec_hbm.at[of], rec_ref.at[of], in_sems.at[p, 0]),
                pltpu.make_async_copy(near_hbm.at[of], near_ref.at[of], in_sems.at[p, 1]),
            )
        )
    for copy in coming[0]:
        copy.start()
    angle = angle_ref[...]
    cosine = jnp.cos(angle)
    sine = jnp.sin(angle)
    interp = interp_ref[...].astype(F32).T

    def matrix(c):
        ci = (cosine[c : c + 1] * interp).astype(BF16)
        si = (sine[c : c + 1] * interp).astype(BF16)
        w_ref[c * 256 : c * 256 + 128, :half] = ci
        w_ref[c * 256 : c * 256 + 128, half:] = si
        w_ref[c * 256 + 128 : c * 256 + 256, :half] = -si
        w_ref[c * 256 + 128 : c * 256 + 256, half:] = ci

    going = []
    for p in range(parents):
        z = separate(z_ref[:, p * 256 : (p + 1) * 256].astype(F32)).astype(BF16)
        pieces = 8
        for n in range(pieces):
            if p == 0:
                for c in range(n * 8 // pieces, (n + 1) * 8 // pieces):
                    matrix(c)
            rows = slice(n * 2048 // pieces, (n + 1) * 2048 // pieces)
            arr_ref[p % 2, rows, :] = dot(w_ref[rows, :], z).astype(BF16)
        for copy in coming[p]:
            copy.wait()
        if p + 1 < parents:
            for copy in coming[p + 1]:
                copy.start()
        for c in range(8):
            box = p * 8 + c
            arriving = arr_ref[p % 2, c * 256 : (c + 1) * 256, :]
            far = dot(embedded(rec_ref[box, 0], rec_ref[box, 1]), arriving)
            out_ref[:, box] = (far + near_ref[box].astype(F32)).astype(BF16).reshape(2, 128, 256)
            if c % 4 == 3:
                of = pl.ds(box - 3, 4)
                going.append(
                    pltpu.make_async_copy(
                        out_ref.at[:, of], out_hbm.at[:, of], out_sems.at[box // 4]
                    )
                )
                going[-1].start()
    for copy in going:
        copy.wait()


def downward(z, interp, angle, receive, near_field):
    boxes = receive.shape[0]
    response = (2, boxes, 128, 256)
    return pl.pallas_call(
        downward_kernel,
        in_specs=[pl.BlockSpec(memory_space=pltpu.VMEM)] * 3
        + [pl.BlockSpec(memory_space=pltpu.HBM)] * 2,
        out_specs=pl.BlockSpec(memory_space=pltpu.HBM),
        out_shape=jax.ShapeDtypeStruct(response, BF16),
        scratch_shapes=[
            pltpu.VMEM(receive.shape, BF16),
            pltpu.VMEM(near_field.shape, BF16),
            pltpu.VMEM((2048, 2 * interp.shape[0]), BF16),
            pltpu.VMEM((2, 2048, 256), BF16),
            pltpu.VMEM(response, BF16),
            pltpu.SemaphoreType.DMA((boxes // 8, 2)),
            pltpu.SemaphoreType.DMA((boxes // 4,)),
        ],
        compiler_params=pltpu.CompilerParams(vmem_limit_bytes=32 * MIB),
        cost_estimate=pl.CostEstimate(flops=5_000_000_000, bytes_accessed=13_000_000, transcendentals=0),
        name="downward",
    )(
        z,
        interp,
        angle,
        pltpu.with_memory_space_constraint(receive, pltpu.HBM),
        pltpu.with_memory_space_constraint(near_field, pltpu.HBM),
    )


def exchanged(value):
    return lax.all_to_all(value, AXES, split_axis=0, concat_axis=0, tiled=True)


def local(
    currents,
    near_tiles,
    near_index,
    near_count,
    radiate,
    receive,
    interp,
    shift_angle,
    far_index,
    far_count,
    trans_index,
    translators,
):
    boxes = currents.shape[1]
    reach = boxes // 2
    sent, leading, trailing = upward(currents, radiate, interp, shift_angle)
    by_direction = exchanged(sent)
    lower = passed_along(trailing, AXES, 1)
    upper = passed_along(leading, AXES, -1)

    table = translators.transpose(2, 1, 0).reshape(8, -1)
    table = jnp.pad(table, ((0, 0), (0, -table.shape[1] % 128)))
    matrix, rest = operators(far_index.T, trans_index.T, far_count[None, :], table)

    back = translate(by_direction, matrix, rest)
    incoming = exchanged(back)

    first = lax.axis_index(AXES) * boxes - reach
    near_field = near(
        (near_index - first).reshape(-1), near_count, lower, currents, upper, near_tiles
    )
    return downward(incoming, interp, shift_angle, receive, near_field)


def solution(mesh):
    placed = (
        P(None, AXES, None, None),
        P(AXES, None, None, None, None),
        P(AXES, None),
        P(AXES),
        P(AXES, None, None, None),
        P(AXES, None, None, None),
        P(),
        P(),
        P(),
        P(),
        P(),
        P(None, None, AXES),
    )
    return jax.shard_map(
        local,
        mesh=mesh,
        in_specs=placed,
        out_specs=P(None, AXES, None, None),
        check_vma=False,
    )
```
